256 devices in a mesh: section: 2 (over core), mp: 4 (over x), dp: 32 (over z, y).
Axes of the slice: x: 4, y: 4, z: 8, core: 2. Of those that a mesh axis runs over, the one named last changes fastest.
Arguments:
- dec_input: bfloat16 [32, 128, 4096], P('dp', 'mp'), may hold values from -6 to 6
- enc_out: bfloat16 [32, 128, 4096], P('dp', ('section', 'mp')), may hold values from -6 to 6
- dec_segment: int32 [32, 128], P('dp'), may hold values from 0 to 3, never falling along the last dimension, each value on 1 to 64 neighbouring positions
- enc_segment: int32 [32, 128], P('dp'), may hold values from 0 to 3, never falling along the last dimension, each value on 1 to 64 neighbouring positions
- norm_gain: float32 [2, 4096], P('section'), may hold values from 0.25 to 1.75
- w_query: bfloat16 [2, 4096, 2048], P('section', 'dp', 'mp'), may hold values from -0.09375 to 0.09375
- w_key: bfloat16 [2, 4096, 2048], P('section', 'dp', 'mp'), may hold values from -0.09375 to 0.09375
- w_value: bfloat16 [2, 4096, 2048], P('section', 'dp', 'mp'), may hold values from -0.09375 to 0.09375
- w_out: bfloat16 [2, 2048, 4096], P('section', 'mp', 'dp'), may hold values from -0.125 to 0.125
- cotangent: bfloat16 [32, 128, 4096], P('dp', 'mp'), may hold values from -6 to 6
Outputs:
- phase_out: bfloat16 [2, 32, 128, 4096], P('section', 'dp', 'mp')
- stream_grad: bfloat16 [2, 32, 128, 4096], P('section', 'dp', 'mp')
- memory_grad: float32 [32, 128, 4096], P('dp', ('section', 'mp'))
The draws below stay inside these ranges and needn't reach their ends.
Inputs may be any that keep to these rules, and one draw needn't show every extreme that they name: Each replica's rows of dec_segment never fall and name each of the 4 samples at least once. `enc_segment`: as dec_segment, over the encoder rows.
All inputs are finite; a program needn't handle non-finite values.
Results may differ from the reference program's by a relative error of at most 0.03.
Values may be sent and summed in bfloat16 or wider, within the bound.
A program may use at most 64 MiB of HBM per device.

```python
import math
import jax
import jax.numpy as jnp
import numpy as np
from jax import lax

D = 4096
DK = 256
SAMPLES = 4
HDIM = 2048
DEC = 128
ENC = 128
REPLICAS = 32
N_SECTION = 2


def levels(stream_key, extent, pieces, smallest, high):
    def one(position, shards_of):
        draws = jax.random.uniform(jax.random.fold_in(jax.random.fold_in(stream_key, 6), position), (shards_of,), jnp.float32, smallest / len(pieces), high / len(pieces))
        return jnp.repeat(jnp.exp(draws), extent[position] // shards_of).reshape((-1,) + (1,) * (len(extent) - position - 1))

    factor_of = one(*pieces[0])
    for cut in pieces[1:]:
        factor_of = factor_of * one(*cut)
    return factor_of


def length_profile(count, total, limit, skew):
    loads = [(1 << 20) // math.isqrt(standing ** skew) + 1 for standing in range(2, count + 1)]
    surplus, counts = total - limit - (count - 1), [1] * (count - 1)
    while surplus > 0:
        movable = [i for i in range(count - 1) if counts[i] < limit]
        whole, budget = sum([loads[i] for i in movable]), surplus
        for i in movable:
            more = min(limit - counts[i], max(1, budget * loads[i] // whole), surplus)
            counts[i] = counts[i] + more
            surplus = surplus - more
    return np.array([limit] + counts)


def ragged(own_key, amount, total, bound, lean):
    if amount == 2:
        one = jax.random.randint(own_key, (), max(1, total - bound), min(bound, total - 1) + 1)
        return jnp.stack([one, total - one])
    sizes = jnp.asarray(length_profile(amount, total, bound, lean), jnp.int32)
    pairs = (amount - 1) // 2
    donor, sink = sizes[1:1 + 2 * pairs:2], sizes[2:2 + 2 * pairs:2]
    room = jnp.minimum(donor - 1, bound - sink)
    shifted = jax.random.randint(jax.random.fold_in(own_key, 1), (pairs,), 0, 1 << 20) % (room + 1)
    sizes = sizes.at[1:1 + 2 * pairs:2].set(donor - shifted).at[2:2 + 2 * pairs:2].set(sink + shifted)
    return sizes[jax.random.permutation(jax.random.fold_in(own_key, 2), amount)]


def noise(stream_key, dims, deviation, bound, pieces=(), dtype=jnp.bfloat16):
    drawn = jax.random.normal(stream_key, dims, jnp.float32) * deviation
    if len(pieces) > 0:
        drawn = levels(stream_key, dims, pieces, -0.22, 0.18) * drawn
    return jnp.clip(drawn, min=-bound, max=bound).astype(dtype)


def setup_inputs(seed: int = 0) -> dict:
    arg_keys = jax.random.split(jax.random.key(seed), 11)
    dec_input = noise(arg_keys[0], (REPLICAS, DEC, D), 1.0, 6.0, ((0, 32), (1, 4)))
    enc_out = noise(arg_keys[1], (REPLICAS, ENC, D), 1.0, 6.0, ((0, 32), (1, 8)))
    dec_segment = jax.vmap(lambda own: jnp.searchsorted(jnp.cumsum(ragged(own, SAMPLES, DEC, DEC // 2, 2)), jnp.arange(DEC), side="right"))(jax.random.split(arg_keys[2], REPLICAS)).reshape((REPLICAS, DEC)).astype(jnp.int32)
    enc_segment = jax.vmap(lambda own: jnp.searchsorted(jnp.cumsum(ragged(own, SAMPLES, ENC, ENC // 2, 2)), jnp.arange(ENC), side="right"))(jax.random.split(arg_keys[3], REPLICAS)).reshape((REPLICAS, ENC)).astype(jnp.int32)
    norm_gain = jnp.clip(1.0 + 0.15 * jax.random.normal(arg_keys[4], (N_SECTION, D), jnp.float32), 0.25, 1.75)
    w_query = noise(arg_keys[5], (N_SECTION, D, HDIM), D ** -0.5, 0.09375, ((0, 2), (1, 32), (2, 4)))
    w_key = noise(arg_keys[6], (N_SECTION, D, HDIM), D ** -0.5, 0.09375, ((0, 2), (1, 32), (2, 4)))
    w_value = noise(arg_keys[7], (N_SECTION, D, HDIM), D ** -0.5, 0.09375, ((0, 2), (1, 32), (2, 4)))
    w_out = noise(arg_keys[8], (N_SECTION, HDIM, D), HDIM ** -0.5, 0.125, ((0, 2), (1, 4), (2, 32)))
    cotangent = noise(arg_keys[9], (REPLICAS, DEC, D), 1.0, 6.0, ((0, 32), (1, 4)))
    return dict(dec_input=dec_input, enc_out=enc_out, dec_segment=dec_segment, enc_segment=enc_segment, norm_gain=norm_gain, w_query=w_query, w_key=w_key, w_value=w_value, w_out=w_out, cotangent=cotangent)


norm_eps = 1e-06

def inverse_rms(values):
    return lax.rsqrt(lax.optimization_barrier(jnp.mean(values * values, axis=-1, keepdims=True)) + norm_eps)

def split_heads(tensor, batch, rows_count, head_count):
    return tensor.reshape(batch, rows_count, head_count, DK).transpose(0, 2, 1, 3).astype(jnp.float32)

def merge_heads(tensor):
    batch, head_count, rows_count, depth = tensor.shape
    return tensor.transpose(0, 2, 1, 3).reshape(batch * rows_count, head_count * depth)

def reference(dec_input, enc_out, dec_segment, enc_segment, norm_gain, w_query, w_key, w_value, w_out, cotangent):
    batch, dec_rows, model_width = dec_input.shape
    enc_rows = enc_out.shape[1]
    head_count = w_query.shape[2] // DK
    score_scale = DK ** (-0.5)
    same_sample = (dec_segment[:, :, None] == enc_segment[:, None, :])[:, None]
    memory_flat = enc_out.reshape(batch * enc_rows, model_width)
    stream = dec_input
    saved = []
    phase_outputs = []
    for phase_step in range(N_SECTION):
        widened = stream.astype(jnp.float32)
        inverse = inverse_rms(widened)
        hidden = (widened * inverse * norm_gain[phase_step]).astype(jnp.bfloat16)
        query = (jnp.dot(hidden.reshape(batch * dec_rows, model_width), w_query[phase_step], preferred_element_type=jnp.float32) * score_scale).astype(jnp.bfloat16)
        keys = jnp.dot(memory_flat, w_key[phase_step], preferred_element_type=jnp.float32).astype(jnp.bfloat16)
        values = jnp.dot(memory_flat, w_value[phase_step], preferred_element_type=jnp.float32).astype(jnp.bfloat16)
        query_heads = split_heads(query, batch, dec_rows, head_count)
        key_heads = split_heads(keys, batch, enc_rows, head_count)
        value_heads = split_heads(values, batch, enc_rows, head_count)
        scores = jnp.einsum('bhrk,bhek->bhre', query_heads, key_heads)
        scores = jnp.where(same_sample, scores, -1e+30)
        row_max = lax.optimization_barrier(jnp.max(scores, axis=-1, keepdims=True))
        weights = jnp.exp(scores - row_max)
        prob = weights / lax.optimization_barrier(jnp.sum(weights, axis=-1, keepdims=True))
        prob_low = prob.astype(jnp.bfloat16)
        attended = merge_heads(jnp.einsum('bhre,bhek->bhrk', prob_low.astype(jnp.float32), value_heads)).astype(jnp.bfloat16)
        update = jnp.dot(attended, w_out[phase_step], preferred_element_type=jnp.float32).reshape(batch, dec_rows, model_width)
        result = (widened + update).astype(jnp.bfloat16)
        saved.append((widened, inverse, query_heads, key_heads, value_heads, prob, prob_low))
        phase_outputs.append(result)
        stream = result
    grad = cotangent
    memory_grad = jnp.zeros((batch * enc_rows, model_width), jnp.float32)
    stream_grads = [None] * N_SECTION
    for phase_step in reversed(range(N_SECTION)):
        widened, inverse, query_heads, key_heads, value_heads, prob, prob_low = saved[phase_step]
        grad_flat = grad.reshape(batch * dec_rows, model_width)
        attended_grad = jnp.dot(grad_flat, w_out[phase_step].T, preferred_element_type=jnp.float32).astype(jnp.bfloat16)
        attended_heads = split_heads(attended_grad, batch, dec_rows, head_count)
        prob_grad = jnp.einsum('bhrk,bhek->bhre', attended_heads, value_heads)
        value_term = jnp.einsum('bhre,bhrk->bhek', prob_low.astype(jnp.float32), attended_heads)
        score_grad = prob * (prob_grad - lax.optimization_barrier(jnp.sum(prob_grad * prob, axis=-1, keepdims=True)))
        query_grad = (merge_heads(jnp.einsum('bhre,bhek->bhrk', score_grad, key_heads)) * score_scale).astype(jnp.bfloat16)
        key_grad = merge_heads(jnp.einsum('bhre,bhrk->bhek', score_grad, query_heads)).astype(jnp.bfloat16)
        value_grad = merge_heads(value_term).astype(jnp.bfloat16)
        memory_grad = memory_grad + jnp.dot(key_grad, w_key[phase_step].T, preferred_element_type=jnp.float32) + jnp.dot(value_grad, w_value[phase_step].T, preferred_element_type=jnp.float32)
        hidden_grad = jnp.dot(query_grad, w_query[phase_step].T, preferred_element_type=jnp.float32).reshape(batch, dec_rows, model_width)
        weighted = norm_gain[phase_step] * hidden_grad
        norm_grad = inverse * weighted - widened * inverse ** 3 * lax.optimization_barrier(jnp.mean(widened * weighted, axis=-1, keepdims=True))
        grad = (grad.astype(jnp.float32) + norm_grad).astype(jnp.bfloat16)
        stream_grads[phase_step] = grad
    return (jnp.stack(phase_outputs), jnp.stack(stream_grads), memory_grad.reshape(batch, enc_rows, model_width))
```

```python
from types import SimpleNamespace

import jax
import jax.numpy as jnp
from jax import lax
from jax.experimental import pallas as pl
from jax.experimental.pallas import tpu as pltpu
from jax.sharding import PartitionSpec as P

MESH = pl.DeviceIdType.MESH
BF = jnp.bfloat16
F32 = jnp.float32

NX, NY, NZ = 4, 4, 8
D = 4096
DK = 256
COLS = 512
HEADS = COLS // DK
ROWS = 32
EROWS = 16
SL = D // NY
N = 128
EPS = 1e-06
SCALE = DK ** (-0.5)
STAT = 1.0 / (D * SCALE)
Q, K, V, O = range(4)


def vm(*shape, dtype=BF):
    return pltpu.VMEM(shape, dtype)


def dma(*shape):
    return pltpu.SemaphoreType.DMA(shape)


BUFFERS = dict(
    wq=vm(NZ, N, COLS),
    wk=vm(NZ, N, COLS),
    wv=vm(NZ, N, COLS),
    wo=vm(NZ, COLS, N),
    esl=vm(NY, EROWS, SL),
    enc=vm(NY, 2, NX, EROWS, SL),
    sl=vm(NY, ROWS, SL),
    a0=vm(NY, NX, ROWS, SL),
    a1=vm(NY, NX, ROWS, SL),
    dsl=vm(NY, ROWS, SL),
    x0=vm(NY, ROWS, SL),
    c0=vm(NY, ROWS, SL),
    x1=vm(NY, ROWS, SL),
    t1=vm(NY, ROWS, SL),
    t2=vm(NY, ROWS, SL),
    inv0s=vm(ROWS, N, dtype=F32),
    inv0=vm(NY, ROWS, N, dtype=F32),
    inv1=vm(NY, ROWS, N, dtype=F32),
    invx=vm(NX, ROWS, N, dtype=F32),
    gain=vm(8, SL, dtype=F32),
    gain_far=vm(8, SL, dtype=F32),
    mask=vm(N, N, dtype=F32),
    prob=vm(HEADS, N, N, dtype=F32),
    sgt=vm(HEADS, N, N),
    pt=vm(HEADS, N, N),
    q=vm(N, COLS),
    k=vm(N, COLS),
    v=vm(N, COLS),
    ag=vm(N, COLS),
    own_q=vm(N, COLS, dtype=F32),
    own_k=vm(N, COLS, dtype=F32),
    own_v=vm(N, COLS, dtype=F32),
    own_ag=vm(N, COLS, dtype=F32),
    s_q=vm(NY, N, COLS),
    s_k=vm(NY, N, COLS),
    s_v=vm(NY, N, COLS),
    s_ag=vm(NY, N, COLS),
    r_q=vm(NY, N, COLS),
    r_k=vm(NY, N, COLS),
    r_v=vm(NY, N, COLS),
    r_ag=vm(NY, N, COLS),
    at=vm(NY, NX, ROWS, COLS),
    qg=vm(NY, NX, ROWS, COLS),
    kg=vm(NY, 2, NX, EROWS, COLS),
    vg=vm(NY, 2, NX, EROWS, COLS),
    sxa=vm(NX, NY, ROWS, SL),
    sxb=vm(NX, NY, ROWS, SL),
    rxa=vm(NX, NY, ROWS, SL),
    rxb=vm(NX, NY, ROWS, SL),
    ss=vm(NY, NY, ROWS, N, dtype=F32),
    sp=vm(NX, ROWS, N, dtype=F32),
    spr1=vm(NX, ROWS, N, dtype=F32),
    spr0=vm(NX, ROWS, N, dtype=F32),
    sall1=vm(NY, ROWS, N, dtype=F32),
    sall0=vm(NY, ROWS, N, dtype=F32),
    por=vm(NY, ROWS, SL),
    sgr=vm(NY, ROWS, SL),
    mgs=vm(NX, NY, EROWS, SL),
    mgk=vm(NX, NY, EROWS, SL, dtype=F32),
    mgc=vm(NX, NY, EROWS, SL),
    rms=vm(NX, NY, EROWS, SL),
    rm=vm(NX, NY, EROWS, SL),
    mos=vm(NY, EROWS, SL),
    mo=vm(NY, EROWS, SL),
)

COPIES = dict(
    ring=(4, 2, 4),
    enc=(NY, NX),
    sl=(NY, NX),
    dsl=(NY,),
    inv0=(NY,),
    gain=(1,),
    ehalf=(1,),
    c0=(1,),
    pq=(NY,),
    pk=(NY,),
    pv=(NY,),
    pag=(NY,),
    at=(NY,),
    qg=(NY,),
    kg=(NY,),
    vg=(NY,),
    xa=(NX,),
    xb=(NX,),
    a1=(NX,),
    ss=(NY,),
    invx=(NX,),
    inv1=(1,),
    x1=(1,),
    spr1=(NX,),
    spr0=(NX,),
    sall1=(NY,),
    sall0=(NY,),
    por=(NY,),
    por1=(NY,),
    sgr=(NY,),
    sgr0=(NY,),
    mgc1=(1,),
    mgc0=(NX,),
    rm=(NX,),
    mo=(NY,),
)


def nn(a, b):
    return jnp.dot(a, b, preferred_element_type=F32)


def nt(a, b):
    return lax.dot_general(a, b, (((1,), (1,)), ((), ())), preferred_element_type=F32)


def kernel(
    dec, enc_in, dseg, eseg, gain_in, wq_in, wk_in, wv_in, wo_in, cot, out_p, out_s, out_m, *scratch
):
    b = SimpleNamespace(**dict(zip(BUFFERS, scratch)))
    rest = scratch[len(BUFFERS) :]
    c = SimpleNamespace(**dict(zip(COPIES, zip(rest[0::2], rest[1::2]))))
    go = rest[-1]

    s = lax.axis_index("section")
    x = lax.axis_index("mp")
    dp = lax.axis_index("dp")
    y = dp % NY
    z = dp // NY
    far = 1 - s

    def dev(sec, xx, yy, zz=None):
        return {"section": sec, "mp": xx, "dp": (z if zz is None else zz) * NY + yy}

    def copy(name, src, dst, si, ri, device):
        return pltpu.make_async_remote_copy(
            src_ref=src,
            dst_ref=dst,
            send_sem=name[0].at[si],
            recv_sem=name[1].at[ri],
            device_id=device,
            device_id_type=MESH,
        )

    here = dev(s, x, y)

    def got(name, dst, ri):
        copy(name, dst, dst, ri, ri, here).wait_recv()

    def sent(name, src, si):
        copy(name, src, src, si, si, here).wait_send()

    def each(lo, hi, body):
        lax.fori_loop(lo, hi, lambda i, c: (body(i), c)[1], 0)

    def y_send(name, src_of, dst, sec, k):
        yp = (y + k) % NY
        copy(name, src_of(yp), dst.at[y], yp, y, dev(sec, x, yp)).start()

    def y_got(name, dst):
        each(1, NY, lambda k: got(name, dst.at[(y + k) % NY], (y + k) % NY))

    def y_sent(name, src_of, lo=1):
        each(lo, NY, lambda k: sent(name, src_of((y + k) % NY), (y + k) % NY))

    def x_got(name, dst, lo=1):
        each(lo, NX, lambda k: got(name, dst((x + k) % NX), (x + k) % NX))

    def x_sent(name, src, lo=1):
        each(lo, NX, lambda k: sent(name, src((x + k) % NX), (x + k) % NX))

    weights = (b.wq, b.wk, b.wv, b.wo)
    weights_in = (wq_in, wk_in, wv_in, wo_in)

    def part(w, slot, step, way):
        ref = weights[w]
        if step < 3:
            return ref.at[slot]
        half = ref.shape[1] // 2
        return ref.at[slot, pl.ds(way * half, half)]

    def ring_send(w, step):
        for way in range(2):
            slot = (z + NZ - step) % NZ if way == 0 else (z + step) % NZ
            to = (z + 1) % NZ if way == 0 else (z + NZ - 1) % NZ
            ref = part(w, slot, step, way)
            copy(c.ring, ref, ref, (w, way, step), (w, way, step), dev(s, x, y, to)).start()

    def ring_got(w, step):
        for way in range(2):
            slot = (z + NZ - 1 - step) % NZ if way == 0 else (z + 1 + step) % NZ
            got(c.ring, part(w, slot, step, way), (w, way, step))

    def ring_sent():
        for w in range(4):
            for step in range(4):
                for way in range(2):
                    slot = (z + NZ - step) % NZ if way == 0 else (z + step) % NZ
                    sent(c.ring, part(w, slot, step, way), (w, way, step))

    def ring_next(w, step):
        ring_got(w, step - 1)
        ring_send(w, step)

    barrier = pltpu.get_barrier_semaphore()

    def hello(device):
        pl.semaphore_signal(barrier, inc=1, device_id=device, device_id_type=MESH)

    def hello_xy(k):
        t = (NX * y + x + k) % (NX * NY)
        hello(dev(s, t % NX, t // NX))

    each(1, NX * NY, hello_xy)
    hello(dev(s, x, y, (z + 1) % NZ))
    hello(dev(s, x, y, (z + NZ - 1) % NZ))
    each(0, NX, lambda k: hello(dev(far, (x + k) % NX, y)))
    each(1, NY, lambda k: hello(dev(far, x, (y + k) % NY)))

    for w in range(4):
        weights[w][z] = weights_in[w][...]

    def pick(value, yp):
        return jnp.concatenate(
            [value[:, (NY * f + yp) * N : (NY * f + yp + 1) * N] for f in range(NZ)], axis=1
        )

    rows_in = dec[...]
    wide = rows_in.astype(F32)
    inverse = lax.rsqrt(jnp.mean(wide * wide, axis=-1, keepdims=True) + EPS)
    inv_tile = jnp.broadcast_to(inverse, (ROWS, N))
    b.inv0s[...] = inv_tile
    b.inv0[y] = inv_tile
    enc_rows = enc_in[...]

    @pl.when(s == 0)
    def _():
        hidden = (wide * inverse * gain_in[...]).astype(BF)
        for yp in range(NY):
            b.sl[yp] = pick(hidden, yp)

    @pl.when(s == 1)
    def _():
        value = cot[...]
        for yp in range(NY):
            b.sl[yp] = pick(value, yp)

    for yp in range(NY):
        b.dsl[yp] = pick(rows_in, yp)
        b.esl[yp] = pick(enc_rows, yp)
    b.a0[y, x] = b.sl[y]
    b.x0[y] = b.dsl[y]
    b.enc[y, s, x] = b.esl[y]
    for f in range(NZ):
        own_gain = gain_in[:, pl.ds(pl.multiple_of((NY * f + y) * N, N), N)]
        b.gain[:, f * N : (f + 1) * N] = jnp.broadcast_to(own_gain, (8, N))
    dec_ids = jnp.broadcast_to(dseg[...].astype(F32), (N, N)).T
    enc_ids = jnp.broadcast_to(eseg[...].astype(F32), (N, N))
    b.mask[...] = jnp.where(dec_ids == enc_ids, 1.0, 0.0)

    pl.semaphore_wait(barrier, NX * NY - 1 + 2 + NX + NY - 1)

    @pl.when(s == 0)
    def _():
        ring_send(Q, 0)
        ring_send(K, 0)

    def xy_start(name, src, dst):
        def one(k):
            t = (NX * y + x + k) % (NX * NY)
            yp, xp = t // NX, t % NX
            copy(name, src.at[yp], dst, (yp, xp), (y, x), dev(s, xp, yp)).start()

        each(1, NX * NY, one)

    def xy_got(name, dst):
        def one(k):
            t = (NX * y + x + k) % (NX * NY)
            got(name, dst(t // NX, t % NX), (t // NX, t % NX))

        each(1, NX * NY, one)

    def xy_sent(name, src):
        def one(k):
            t = (NX * y + x + k) % (NX * NY)
            sent(name, src.at[t // NX], (t // NX, t % NX))

        each(1, NX * NY, one)

    xy_start(c.sl, b.sl, b.a0.at[y, x])
    xy_start(c.enc, b.esl, b.enc.at[y, s, x])
    each(1, NY, lambda k: y_send(c.dsl, lambda i: b.dsl.at[i], b.x0, s, k))
    each(1, NY, lambda k: y_send(c.inv0, lambda i: b.inv0s, b.inv0, s, k))
    copy(c.gain, b.gain, b.gain_far, 0, 0, dev(far, x, y)).start()

    def enc_half():
        xy_got(c.enc, lambda yp, xp: b.enc.at[yp, s, xp])
        copy(c.ehalf, b.enc.at[:, s], b.enc.at[:, s], 0, 0, dev(far, x, y)).start()

    def enc_whole():
        got(c.ehalf, b.enc.at[:, far], 0)

    def times(w, a):
        return nn(a, weights[w][...].reshape(NZ * N, COLS))

    def pair(p):
        return jnp.concatenate([b.wo[2 * p], b.wo[2 * p + 1]], axis=1)

    def times_out_t(a):
        total = nt(a[:, : 2 * N], pair(0))
        for p in range(1, NZ // 2):
            total += nt(a[:, 2 * N * p : 2 * N * (p + 1)], pair(p))
        return total

    def project(name, rows_of, product, stage, landing, own):
        def one(k):
            yp = (y + k) % NY
            stage[yp] = product(rows_of(yp)).astype(BF)
            y_send(name, lambda i: stage.at[i], landing, s, k)

        each(1, NY, one)
        own[...] = product(rows_of(y))

    def projected(name, landing, own):
        y_got(name, landing)
        total = own[...]
        for k in range(1, NY):
            total += landing[(y + k) % NY].astype(F32)
        return total

    def act(buffer):
        return lambda yp: buffer[yp].reshape(N, SL)

    def head(value, h):
        return value[:, h * DK : (h + 1) * DK]

    def probabilities():
        for h in range(HEADS):
            scores = nt(head(b.q, h), head(b.k, h))
            scores = jnp.where(b.mask[...] > 0.5, scores, -1e30)
            top = jnp.max(scores, axis=-1, keepdims=True)
            e = jnp.exp(scores - top)
            b.prob[h] = e / jnp.sum(e, axis=-1, keepdims=True)

    def attend():
        joined = jnp.concatenate(
            [nn(b.prob[h].astype(BF), head(b.v, h)) for h in range(HEADS)], axis=1
        ).astype(BF)
        b.at[y] = joined.reshape(NX, ROWS, COLS)
        each(1, NY, lambda k: y_send(c.at, lambda i: b.at.at[y], b.at, s, k))

    def query_gradient():
        grads = []
        for h in range(HEADS):
            prob = b.prob[h]
            prob_grad = nt(head(b.ag, h), head(b.v, h))
            score_grad = prob * (prob_grad - jnp.sum(prob_grad * prob, axis=-1, keepdims=True))
            b.sgt[h] = score_grad.T.astype(BF)
            b.pt[h] = prob.T.astype(BF)
            grads.append(nn(score_grad.astype(BF), head(b.k, h)) * SCALE)
        low = jnp.concatenate(grads, axis=1).astype(BF)
        b.qg[y] = low.reshape(NX, ROWS, COLS)
        each(1, NY, lambda k: y_send(c.qg, lambda i: b.qg.at[y], b.qg, s, k))
        both = low.astype(F32) * b.q[...].astype(F32)
        lanes = both[:, :N]
        for f in range(1, COLS // N):
            lanes += both[:, f * N : (f + 1) * N]
        b.sp[...] = lanes.reshape(NX, ROWS, N)

    def key_value_gradients():
        key = jnp.concatenate(
            [nn(b.sgt[h], head(b.q, h)) for h in range(HEADS)], axis=1
        ).astype(BF)
        value = jnp.concatenate(
            [nn(b.pt[h], head(b.ag, h)) for h in range(HEADS)], axis=1
        ).astype(BF)
        b.kg[y] = key.reshape(2, NX, EROWS, COLS)
        b.vg[y] = value.reshape(2, NX, EROWS, COLS)
        each(1, NY, lambda k: y_send(c.kg, lambda i: b.kg.at[y], b.kg, s, k))
        each(1, NY, lambda k: y_send(c.vg, lambda i: b.vg.at[y], b.vg, s, k))

    def update_rows(xp, stage):
        a = b.at[:, xp].reshape(N, COLS)
        for p in range(NZ // 2):
            part_out = nn(a, pair(p)).astype(BF).reshape(NY, ROWS, 2 * N)
            stage[xp, :, :, 2 * N * p : 2 * N * (p + 1)] = part_out

    def hidden_rows(xp, stage):
        a = b.qg[:, xp].reshape(N, COLS)
        for p in range(NZ // 2):
            block = b.wq[2 * p : 2 * p + 2].reshape(2 * N, COLS)
            part_out = nt(a, block).astype(BF).reshape(NY, ROWS, 2 * N)
            stage[xp, :, :, 2 * N * p : 2 * N * (p + 1)] = part_out

    def scatter_x(name, rows_into, stage, landing, sec, keep):
        def one(k):
            xp = (x + k) % NX
            rows_into(xp, stage)
            copy(name, stage.at[xp], landing.at[x], xp, x, dev(sec, xp, y)).start()

        if keep:
            each(1, NX, one)
            rows_into(x, stage)
            landing[x] = stage[x]
        else:
            each(1, NX + 1, one)

    def sum_x(landing, yp):
        total = landing[0, yp].astype(F32)
        for i in range(1, NX):
            total += landing[i, yp].astype(F32)
        return total

    def gather_x():
        def one(k):
            xp = (x + k) % NX
            copy(c.a1, b.a1.at[:, x], b.a1.at[:, x], xp, x, dev(s, xp, y)).start()

        each(1, NX, one)

    def across(tile):
        return jnp.concatenate([tile] * (SL // N), axis=1)

    def send_stat(name, landing, keep):
        def one(k):
            xp = (x + k) % NX
            copy(name, b.sp.at[xp], landing.at[x], xp, x, dev(0, xp, y)).start()

        each(1, NX if keep else NX + 1, one)
        if keep:
            landing[x] = b.sp[x]

    def share_stat(name, landing, result, name_out, lo):
        x_got(name, lambda i: landing.at[i], lo)
        lanes = landing[0] + landing[1] + landing[2] + landing[3]
        result[y] = jnp.broadcast_to(jnp.sum(lanes, axis=-1, keepdims=True), (ROWS, N))
        each(1, NY, lambda k: y_send(name_out, lambda i: result.at[y], result, 0, k))

    def norm_gradient(yp, landing, gain_ref, rows, inv_ref, stat_ref, grad):
        u = sum_x(landing, yp) * gain_ref[0:1, :]
        inv = inv_ref[yp]
        coef = inv * inv * stat_ref[yp] * STAT
        wide_rows = rows[yp].astype(F32)
        return (grad[yp].astype(F32) + across(inv) * u - wide_rows * across(coef)).astype(BF)

    def memory_rows(xp):
        key = b.kg[:, :, xp].reshape(N, COLS)
        value = b.vg[:, :, xp].reshape(N, COLS)
        blocks = []
        for p in range(NZ // 2):
            wk_block = b.wk[2 * p : 2 * p + 2].reshape(2 * N, COLS)
            wv_block = b.wv[2 * p : 2 * p + 2].reshape(2 * N, COLS)
            blocks.append((nt(key, wk_block) + nt(value, wv_block)).reshape(NY, 2, EROWS, 2 * N))
        return blocks

    def lanes_of(p):
        return slice(2 * N * p, 2 * N * (p + 1))

    def send_memory(xp):
        copy(c.rm, b.rms.at[xp], b.rm.at[x], xp, x, dev(s, xp, y)).start()

    @pl.when(s == 0)
    def _():
        ring_next(Q, 1)
        ring_next(K, 1)
        enc_half()
        ring_next(Q, 2)
        ring_next(K, 2)
        ring_send(V, 0)
        ring_send(O, 0)
        ring_next(Q, 3)
        ring_next(K, 3)
        xy_got(c.sl, lambda yp, xp: b.a0.at[yp, xp])
        ring_next(V, 1)
        ring_next(O, 1)
        ring_got(Q, 3)
        project(c.pq, act(b.a0), lambda a: times(Q, a), b.s_q, b.r_q, b.own_q)
        ring_next(V, 2)
        ring_next(O, 2)
        enc_whole()
        ring_got(K, 3)
        project(c.pk, act(b.enc), lambda a: times(K, a), b.s_k, b.r_k, b.own_k)
        ring_next(V, 3)
        ring_next(O, 3)
        pl.semaphore_signal(go, inc=1, device_id=dev(1, x, y), device_id_type=MESH)
        b.q[...] = (projected(c.pq, b.r_q, b.own_q) * SCALE).astype(BF)
        ring_got(V, 3)
        project(c.pv, act(b.enc), lambda a: times(V, a), b.s_v, b.r_v, b.own_v)
        b.k[...] = projected(c.pk, b.r_k, b.own_k).astype(BF)
        probabilities()
        b.v[...] = projected(c.pv, b.r_v, b.own_v).astype(BF)
        attend()
        ring_got(O, 3)
        y_got(c.at, b.at)
        scatter_x(c.xa, update_rows, b.sxa, b.rxa, 1, False)

        got(c.gain, b.gain_far, 0)
        got(c.c0, b.c0, 0)
        got(c.x1, b.x1, 0)
        got(c.inv1, b.inv1, 0)
        y_got(c.dsl, b.x0)
        y_got(c.inv0, b.inv0)
        share_stat(c.spr1, b.spr1, b.sall1, c.sall1, 0)
        y_got(c.sall1, b.sall1)
        x_got(c.xa, lambda i: b.rxa.at[i], 0)

        def grad_one(yp):
            g = norm_gradient(
                yp, b.rxa, b.gain_far, b.x1, b.inv1, b.sall1, b.c0
            )
            b.t1[yp] = g
            b.a1[yp, x] = g

        each(0, NY, grad_one)
        gather_x()
        each(1, NY + 1, lambda k: y_send(c.sgr, lambda i: b.t1.at[i], b.sgr, 1, k))

        x_got(c.a1, lambda i: b.a1.at[:, i])
        project(c.pag, act(b.a1), times_out_t, b.s_ag, b.r_ag, b.own_ag)
        b.ag[...] = projected(c.pag, b.r_ag, b.own_ag).astype(BF)
        query_gradient()
        send_stat(c.spr0, b.spr0, True)
        key_value_gradients()
        y_got(c.qg, b.qg)
        scatter_x(c.xb, hidden_rows, b.sxb, b.rxb, 0, True)
        share_stat(c.spr0, b.spr0, b.sall0, c.sall0, 1)
        y_got(c.kg, b.kg)
        y_got(c.vg, b.vg)
        got(c.mgc1, b.mgc, 0)

        def memory_one(k):
            xp = (x + k) % NX
            for p, block in enumerate(memory_rows(xp)):
                b.mgs[xp, :, :, lanes_of(p)] = block[:, 1].astype(BF)
                kept = block[:, 0] + b.mgc[xp, :, :, lanes_of(p)].astype(F32)
                b.rms[xp, :, :, lanes_of(p)] = kept.astype(BF)
            copy(c.mgc0, b.mgs.at[xp], b.mgc.at[xp], xp, xp, dev(1, x, y)).start()

        def memory_send(k):
            memory_one(k)
            send_memory((x + k) % NX)

        each(1, NX, memory_send)
        memory_one(NX)
        b.rm[x] = b.rms[x]

        y_got(c.sall0, b.sall0)
        x_got(c.xb, lambda i: b.rxb.at[i])

        def grad_zero(yp):
            b.t2[yp] = norm_gradient(
                yp, b.rxb, b.gain, b.x0, b.inv0, b.sall0, b.t1
            )

        each(0, NY, grad_zero)
        each(1, NY, lambda k: y_send(c.sgr0, lambda i: b.t2.at[i], b.sgr, 0, k))
        b.sgr[y] = b.t2[y]

    @pl.when(s == 1)
    def _():
        enc_half()
        xy_got(c.sl, lambda yp, xp: b.a0.at[yp, xp])
        copy(c.c0, b.a0.at[:, x], b.c0, 0, 0, dev(0, x, y)).start()
        y_got(c.dsl, b.x0)
        y_got(c.inv0, b.inv0)
        got(c.gain, b.gain_far, 0)
        enc_whole()
        pl.semaphore_wait(go, 1)
        ring_send(K, 0)
        ring_send(V, 0)
        ring_next(K, 1)
        ring_next(V, 1)
        ring_next(K, 2)
        ring_next(V, 2)
        ring_send(O, 0)
        ring_send(Q, 0)
        ring_next(K, 3)
        ring_next(V, 3)
        ring_next(O, 1)
        ring_next(Q, 1)
        ring_got(K, 3)
        project(c.pk, act(b.enc), lambda a: times(K, a), b.s_k, b.r_k, b.own_k)
        ring_next(O, 2)
        ring_next(Q, 2)
        ring_got(V, 3)
        project(c.pv, act(b.enc), lambda a: times(V, a), b.s_v, b.r_v, b.own_v)
        ring_next(O, 3)
        ring_next(Q, 3)
        b.k[...] = projected(c.pk, b.r_k, b.own_k).astype(BF)
        b.v[...] = projected(c.pv, b.r_v, b.own_v).astype(BF)
        ring_got(O, 3)
        project(c.pag, act(b.a0), times_out_t, b.s_ag, b.r_ag, b.own_ag)
        b.ag[...] = projected(c.pag, b.r_ag, b.own_ag).astype(BF)
        ring_got(Q, 3)

        x_got(c.xa, lambda i: b.rxa.at[i], 0)

        def stream_one(yp):
            rows = (b.x0[yp].astype(F32) + sum_x(b.rxa, yp)).astype(BF)
            b.x1[yp] = rows
            rows = rows.astype(F32)
            b.a1[yp, x] = (rows * b.gain[0:1, :]).astype(BF)
            squares = rows * rows
            lanes = squares[:, :N]
            for f in range(1, SL // N):
                lanes += squares[:, f * N : (f + 1) * N]
            b.ss[y, yp] = lanes

        each(0, NY, stream_one)
        gather_x()
        each(1, NY, lambda k: y_send(c.ss, lambda i: b.ss.at[y], b.ss, 1, k))
        copy(c.x1, b.x1, b.x1, 0, 0, dev(0, x, y)).start()
        each(1, NY + 1, lambda k: y_send(c.por, lambda i: b.x1.at[i], b.por, 0, k))
        y_got(c.ss, b.ss)

        def inverse_one(yp):
            lanes = b.ss[0, yp] + b.ss[1, yp] + b.ss[2, yp] + b.ss[3, yp]
            inv = lax.rsqrt(jnp.sum(lanes, axis=-1, keepdims=True) * (1.0 / D) + EPS)
            b.inv1[yp] = jnp.broadcast_to(inv, (ROWS, N))

        each(0, NY, inverse_one)
        b.invx[x] = b.inv1[y]

        def invx_one(k):
            xp = (x + k) % NX
            copy(c.invx, b.inv1.at[y], b.invx.at[x], xp, x, dev(1, xp, y)).start()

        each(1, NX, invx_one)
        copy(c.inv1, b.inv1, b.inv1, 0, 0, dev(0, x, y)).start()
        x_got(c.a1, lambda i: b.a1.at[:, i])
        project(c.pq, act(b.a1), lambda a: times(Q, a), b.s_q, b.r_q, b.own_q)
        x_got(c.invx, lambda i: b.invx.at[i])
        row_scale = b.invx[...].reshape(N, N) * SCALE
        row_scale = jnp.concatenate([row_scale] * (COLS // N), axis=1)
        b.q[...] = (projected(c.pq, b.r_q, b.own_q) * row_scale).astype(BF)
        probabilities()
        query_gradient()
        send_stat(c.spr1, b.spr1, False)
        y_got(c.qg, b.qg)
        scatter_x(c.xa, hidden_rows, b.sxa, b.rxa, 0, False)

        attend()
        key_value_gradients()
        y_got(c.at, b.at)
        scatter_x(c.xb, update_rows, b.sxb, b.rxb, 1, True)
        y_got(c.kg, b.kg)
        y_got(c.vg, b.vg)

        def memory_one(xp):
            for p, block in enumerate(memory_rows(xp)):
                b.mgs[xp, :, :, lanes_of(p)] = block[:, 0].astype(BF)
                b.mgk[xp, :, :, lanes_of(p)] = block[:, 1]

        each(0, NX, memory_one)
        copy(c.mgc1, b.mgs, b.mgc, 0, 0, dev(0, x, y)).start()
        x_got(c.xb, lambda i: b.rxb.at[i])

        def output_one(yp):
            b.t2[yp] = (b.x1[yp].astype(F32) + sum_x(b.rxb, yp)).astype(BF)

        each(0, NY, output_one)
        each(1, NY, lambda k: y_send(c.por1, lambda i: b.t2.at[i], b.por, 1, k))
        b.por[y] = b.t2[y]

        def memory_send(k):
            xp = (x + k) % NX
            got(c.mgc0, b.mgc.at[xp], xp)
            b.rms[xp] = (b.mgk[xp] + b.mgc[xp].astype(F32)).astype(BF)

            @pl.when(k < NX)
            def _():
                send_memory(xp)

        each(1, NX + 1, memory_send)
        b.rm[x] = b.rms[x]

    x_got(c.rm, lambda i: b.rm.at[i])
    total = b.rm[0].astype(F32)
    for i in range(1, NX):
        total += b.rm[i].astype(F32)
    b.mos[...] = total.astype(BF)
    each(1, NY, lambda k: y_send(c.mo, lambda i: b.mos.at[i], b.mo, s, k))
    b.mo[y] = b.mos[y]

    def whole(landing, out):
        for yp in range(NY):
            value = landing[yp]
            for f in range(NZ):
                at = (NY * f + yp) * N
                out[:, at : at + N] = value[:, f * N : (f + 1) * N].astype(out.dtype)

    @pl.when(s == 0)
    def _():
        each(0, NY, lambda i: got(c.por, b.por.at[i], i))
        y_got(c.sgr0, b.sgr)

    @pl.when(s == 1)
    def _():
        y_got(c.por1, b.por)
        each(0, NY, lambda i: got(c.sgr, b.sgr.at[i], i))

    whole(b.por, out_p)
    whole(b.sgr, out_s)
    y_got(c.mo, b.mo)
    whole(b.mo, out_m)

    ring_sent()
    xy_sent(c.sl, b.sl)
    xy_sent(c.enc, b.esl)
    y_sent(c.dsl, lambda i: b.dsl.at[i])
    y_sent(c.inv0, lambda i: b.inv0s)
    sent(c.gain, b.gain, 0)
    sent(c.ehalf, b.enc.at[:, s], 0)
    for name, stage in ((c.pq, b.s_q), (c.pk, b.s_k), (c.pv, b.s_v), (c.pag, b.s_ag)):
        y_sent(name, lambda i, stage=stage: stage.at[i])
    for name, stage in ((c.at, b.at), (c.qg, b.qg), (c.kg, b.kg), (c.vg, b.vg)):
        y_sent(name, lambda i, stage=stage: stage.at[y])
    x_sent(c.rm, lambda i: b.rms.at[i])
    y_sent(c.mo, lambda i: b.mos.at[i])
    x_sent(c.a1, lambda i: b.a1.at[:, x])
    x_sent(c.xa, lambda i: b.sxa.at[i], 0)
    x_sent(c.xb, lambda i: b.sxb.at[i])

    @pl.when(s == 0)
    def _():
        y_sent(c.sgr, lambda i: b.t1.at[i], 0)
        y_sent(c.sgr0, lambda i: b.t2.at[i])
        y_sent(c.sall1, lambda i: b.sall1.at[y])
        y_sent(c.sall0, lambda i: b.sall0.at[y])
        x_sent(c.spr0, lambda i: b.sp.at[i])
        x_sent(c.mgc0, lambda i: b.mgs.at[i], 0)

    @pl.when(s == 1)
    def _():
        sent(c.c0, b.a0.at[:, x], 0)
        y_sent(c.por, lambda i: b.x1.at[i], 0)
        y_sent(c.por1, lambda i: b.t2.at[i])
        sent(c.x1, b.x1, 0)
        sent(c.inv1, b.inv1, 0)
        sent(c.mgc1, b.mgs, 0)
        y_sent(c.ss, lambda i: b.ss.at[y])
        x_sent(c.invx, lambda i: b.inv1.at[y])
        x_sent(c.spr1, lambda i: b.sp.at[i], 0)


def body(*args):
    dec, enc, dseg, eseg, gain, wq, wk, wv, wo, cot = args
    sems = []
    for shape in COPIES.values():
        sems += [dma(*shape), dma(*shape)]
    phase, stream, memory = pl.pallas_call(
        kernel,
        out_shape=(
            jax.ShapeDtypeStruct((ROWS, D), BF),
            jax.ShapeDtypeStruct((ROWS, D), BF),
            jax.ShapeDtypeStruct((EROWS, D), F32),
        ),
        in_specs=[pl.BlockSpec(memory_space=pltpu.VMEM)] * 10,
        out_specs=(pl.BlockSpec(memory_space=pltpu.VMEM),) * 3,
        scratch_shapes=list(BUFFERS.values()) + sems + [pltpu.SemaphoreType.REGULAR],
        compiler_params=pltpu.CompilerParams(
            collective_id=0, has_side_effects=True, vmem_limit_bytes=56 * 2**20
        ),
        cost_estimate=pl.CostEstimate(
            flops=16 * 2**30, bytes_accessed=4 * 2**20, transcendentals=2**16
        ),
        name="decoder_phases",
    )(dec[0], enc[0], dseg, eseg, gain, wq[0], wk[0], wv[0], wo[0], cot[0])
    return phase[None, None], stream[None, None], memory[None]


def solution(mesh):
    in_specs = (
        P("dp", "mp", None),
        P("dp", ("section", "mp"), None),
        P("dp", None),
        P("dp", None),
        P("section", None),
        P("section", "dp", "mp"),
        P("section", "dp", "mp"),
        P("section", "dp", "mp"),
        P("section", "mp", "dp"),
        P("dp", "mp", None),
    )
    out_specs = (
        P("section", "dp", "mp", None),
        P("section", "dp", "mp", None),
        P("dp", ("section", "mp"), None),
    )
    return jax.shard_map(body, mesh=mesh, in_specs=in_specs, out_specs=out_specs, check_vma=False)
```

```python
from types import SimpleNamespace

import jax
import jax.numpy as jnp
from jax import lax
from jax.experimental import pallas as pl
from jax.experimental.pallas import tpu as pltpu
from jax.sharding import PartitionSpec as P

MESH = pl.DeviceIdType.MESH
BF = jnp.bfloat16
F32 = jnp.float32

NX, NY, NZ = 4, 4, 8
NXY = NX * NY
D = 4096
DK = 256
COLS = 512
HEADS = COLS // DK
ROWS = 32
EROWS = 16
SL = D // NY
N = 128
EPS = 1e-06
SCALE = DK ** (-0.5)
STAT = 1.0 / (D * SCALE)
Q, K, V, O = range(4)
ORDER = (0, 1, 3, 2)


def vm(*shape, dtype=BF):
    return pltpu.VMEM(shape, dtype)


BUFFERS = dict(
    wq=vm(NZ, N, COLS),
    wk=vm(NZ, N, COLS),
    wv=vm(NZ, N, COLS),
    wo=vm(NZ, COLS, N),
    dec=vm(ROWS, D),
    enc_in=vm(EROWS, D),
    cot=vm(ROWS, D),
    gain_in=vm(1, D, dtype=F32),
    dseg=vm(1, N, dtype=jnp.int32),
    eseg=vm(1, N, dtype=jnp.int32),
    esl=vm(NY, EROWS, SL),
    enc=vm(2 * NXY, EROWS, SL),
    sl=vm(NY, ROWS, SL),
    a0=vm(NXY, ROWS, SL),
    a1=vm(NXY, ROWS, SL),
    dsl=vm(NY, ROWS, SL),
    x0=vm(NY, ROWS, SL),
    c0=vm(NY, ROWS, SL),
    x1=vm(NY, ROWS, SL),
    t1=vm(NY, ROWS, SL),
    t2=vm(NY, ROWS, SL),
    inv0s=vm(ROWS, N, dtype=F32),
    inv0=vm(NY, ROWS, N, dtype=F32),
    inv1=vm(NY, ROWS, N, dtype=F32),
    invx=vm(NX, ROWS, N, dtype=F32),
    gain=vm(8, SL, dtype=F32),
    gain_far=vm(8, SL, dtype=F32),
    mask=vm(N, N, dtype=F32),
    prob=vm(HEADS, N, N, dtype=F32),
    sgt=vm(HEADS, N, N),
    pt=vm(HEADS, N, N),
    q=vm(N, COLS),
    k=vm(N, COLS),
    v=vm(N, COLS),
    ag=vm(N, COLS),
    own_q=vm(N, COLS, dtype=F32),
    own_k=vm(N, COLS, dtype=F32),
    own_v=vm(N, COLS, dtype=F32),
    own_ag=vm(N, COLS, dtype=F32),
    s_q=vm(NY, N, COLS),
    s_k=vm(NY, N, COLS),
    s_v=vm(NY, N, COLS),
    s_ag=vm(NY, N, COLS),
    r_q=vm(NY, N, COLS),
    r_k=vm(NY, N, COLS),
    r_v=vm(NY, N, COLS),
    r_ag=vm(NY, N, COLS),
    at=vm(NY, N, COLS),
    qg=vm(NY, N, COLS),
    kg=vm(NY, N, COLS),
    vg=vm(NY, N, COLS),
    sxa=vm(NXY, ROWS, SL),
    sxb=vm(NXY, ROWS, SL),
    rxa=vm(NXY, ROWS, SL),
    rxb=vm(NXY, ROWS, SL),
    ss=vm(NY, NY, ROWS, N, dtype=F32),
    sp=vm(NX, ROWS, N, dtype=F32),
    spr1=vm(NX, ROWS, N, dtype=F32),
    spr0=vm(NX, ROWS, N, dtype=F32),
    sall1=vm(NY, ROWS, N, dtype=F32),
    sall0=vm(NY, ROWS, N, dtype=F32),
    por=vm(NY, ROWS, SL),
    sgr=vm(NY, ROWS, SL),
    mgs=vm(2 * NXY, EROWS, SL),
    mgc=vm(2 * NXY, EROWS, SL),
    rm=vm(NXY, EROWS, SL),
    mos=vm(NY, EROWS, SL),
    mo=vm(NY, EROWS, SL),
)

COPIES = dict(
    ring_q=(2, 4),
    ring_k=(2, 4),
    ring_v=(2, 4),
    ring_o=(2, 4),
    enc=(1,),
    sl=(1,),
    dsl=(1,),
    inv0=(1,),
    gain=(1,),
    ehalf=(1,),
    c0=(1,),
    pq=(1,),
    pk=(1,),
    pv=(1,),
    pag=(1,),
    at=(NY,),
    qg=(NY,),
    kg=(NY,),
    vg=(NY,),
    xa=(NY,),
    xb=(NY,),
    a1=(NY,),
    ss=(1,),
    invx=(1,),
    inv1=(1,),
    x1=(1,),
    spr1=(1,),
    spr0=(1,),
    sall1=(1,),
    sall0=(1,),
    por=(1,),
    por1=(1,),
    sgr=(1,),
    sgr0=(1,),
    mgc=(NY,),
    rm=(NY,),
    mo=(1,),
)
LOCAL = 13


def nn(a, b):
    return jnp.dot(a, b, preferred_element_type=F32)


def nt(a, b):
    return lax.dot_general(a, b, (((1,), (1,)), ((), ())), preferred_element_type=F32)


def kernel(*refs):
    dec, enc_in, dseg, eseg, gain_in, wq_in, wk_in, wv_in, wo_in, cot = refs[:10]
    out_p, out_s, out_m = refs[10:13]
    scratch = refs[13:]
    b = SimpleNamespace(**dict(zip(BUFFERS, scratch)))
    rest = scratch[len(BUFFERS) :]
    send_sems, local_sems, go = rest[len(COPIES) :]
    c = SimpleNamespace(**{n: (r, i) for i, (n, r) in enumerate(zip(COPIES, rest))})

    s = lax.axis_index("section")
    x = lax.axis_index("mp")
    dp = lax.axis_index("dp")
    y = dp % NY
    z = dp // NY
    far = 1 - s

    def dev(sec, xx, yy, zz=None):
        return {"section": sec, "mp": xx, "dp": (z if zz is None else zz) * NY + yy}

    here = dev(s, x, y)

    def copy(step, src, dst, at, device):
        return pltpu.make_async_remote_copy(
            src_ref=src,
            dst_ref=dst,
            send_sem=send_sems.at[step[1]],
            recv_sem=step[0].at[at],
            device_id=device,
            device_id_type=MESH,
        )

    def got(step, ref, at=0):
        copy(step, ref, ref, at, here).wait_recv()

    def sent(step, ref):
        first = (0,) * len(step[0].shape)
        copy(step, ref, ref, first, here).wait_send()

    def each(lo, hi, body):
        lax.fori_loop(lo, hi, lambda i, carry: (body(i), carry)[1], 0)

    def by_distance(i):
        return i + (i // 2) * (5 - 2 * i)

    def near(k):
        return (y + by_distance(k)) % NY

    def y_send(step, src_of, dst, sec, lo, at=None):
        def one(k):
            yp = (y + k) % NY
            copy(step, src_of(yp), dst.at[y], 0 if at is None else at, dev(sec, x, yp)).start()

        each(lo, NY, one)

    def x_send(step, src_of, dst, sec, lo, at=0):
        def one(k):
            xp = (x + k) % NX
            copy(step, src_of(xp), dst, at, dev(sec, xp, y)).start()

        each(lo, NX, one)

    weights = (b.wq, b.wk, b.wv, b.wo)
    rings = (c.ring_q, c.ring_k, c.ring_v, c.ring_o)

    def part(w, slot, step, way):
        ref = weights[w]
        if step < 3:
            return ref.at[slot]
        half = ref.shape[1] // 2
        return ref.at[slot, pl.ds(way * half, half)]

    def ring_send(w, step):
        for way in range(2):
            slot = (z + NZ - step) % NZ if way == 0 else (z + step) % NZ
            to = (z + 1) % NZ if way == 0 else (z + NZ - 1) % NZ
            ref = part(w, slot, step, way)
            copy(rings[w], ref, ref, (way, step), dev(s, x, y, to)).start()

    def ring_got(w, step):
        for way in range(2):
            slot = (z + NZ - 1 - step) % NZ if way == 0 else (z + 1 + step) % NZ
            got(rings[w], part(w, slot, step, way), (way, step))

    def ring_next(step, *ws):
        for w in ws:
            ring_got(w, step - 1)
            ring_send(w, step)

    barrier = pltpu.get_barrier_semaphore()

    def hello(device):
        pl.semaphore_signal(barrier, inc=1, device_id=device, device_id_type=MESH)

    def hello_xy(k):
        t = (NX * y + x + k) % NXY
        hello(dev(s, t % NX, t // NX))

    each(1, NXY, hello_xy)
    hello(dev(s, x, y, (z + 1) % NZ))
    hello(dev(s, x, y, (z + NZ - 1) % NZ))
    each(0, NX, lambda k: hello(dev(far, (x + k) % NX, y)))
    each(1, NY, lambda k: hello(dev(far, x, (y + k) % NY)))

    def local(src, dst, i):
        return pltpu.make_async_copy(src, dst, local_sems.at[i])

    loads = [
        local(src, dst, i)
        for i, (src, dst) in enumerate(
            (
                (dec, b.dec),
                (gain_in, b.gain_in),
                (enc_in, b.enc_in),
                (dseg, b.dseg),
                (eseg, b.eseg),
                (cot, b.cot),
                (wq_in, b.wq.at[z]),
                (wk_in, b.wk.at[z]),
                (wv_in, b.wv.at[z]),
                (wo_in, b.wo.at[z]),
            )
        )
    ]
    for load in loads:
        load.start()
    for load in loads:
        load.wait()

    def pick(value, yp):
        return jnp.concatenate(
            [value[:, (NY * f + yp) * N : (NY * f + yp + 1) * N] for f in range(NZ)], axis=1
        )

    rows_in = b.dec[...]
    enc_rows = b.enc_in[...]

    @pl.when(s == 0)
    def _():
        wide = rows_in.astype(F32)
        inverse = lax.rsqrt(jnp.mean(wide * wide, axis=-1, keepdims=True) + EPS)
        inv_tile = jnp.broadcast_to(inverse, (ROWS, N))
        b.inv0s[...] = inv_tile
        b.inv0[y] = inv_tile
        hidden = (wide * inverse * b.gain_in[...]).astype(BF)
        for yp in range(NY):
            b.sl[yp] = pick(hidden, yp)

    @pl.when(s == 1)
    def _():
        value = b.cot[...]
        for yp in range(NY):
            b.sl[yp] = pick(value, yp)

    for yp in range(NY):
        b.dsl[yp] = pick(rows_in, yp)
        b.esl[yp] = pick(enc_rows, yp)
    b.a0[NX * y + x] = b.sl[y]
    b.x0[y] = b.dsl[y]
    b.enc[(2 * y + s) * NX + x] = b.esl[y]
    for f in range(NZ):
        own_gain = b.gain_in[:, pl.ds(pl.multiple_of((NY * f + y) * N, N), N)]
        b.gain[:, f * N : (f + 1) * N] = jnp.broadcast_to(own_gain, (8, N))
    dec_ids = jnp.broadcast_to(b.dseg[...].astype(F32), (N, N)).T
    enc_ids = jnp.broadcast_to(b.eseg[...].astype(F32), (N, N))
    b.mask[...] = jnp.where(dec_ids == enc_ids, 1.0, 0.0)

    pl.semaphore_wait(barrier, NXY - 1 + 2 + NX + NY - 1)

    def xy_start(step, src, dst):
        def one(k):
            t = (NX * y + x + k) % NXY
            copy(step, src.at[t // NX], dst, 0, dev(s, t % NX, t // NX)).start()

        each(1, NXY, one)

    def enc_start():
        xy_start(c.enc, b.esl, b.enc.at[(2 * y + s) * NX + x])

    def sl_start():
        xy_start(c.sl, b.sl, b.a0.at[NX * y + x])

    def small_start():
        copy(c.gain, b.gain, b.gain_far, 0, dev(far, x, y)).start()
        y_send(c.dsl, lambda i: b.dsl.at[i], b.x0, s, 1)

    def enc_half():
        got(c.enc, b.enc.at[pl.ds(0, NXY - 1)])
        for yp in range(NY):
            block = b.enc.at[pl.ds((2 * yp + s) * NX, NX)]
            copy(c.ehalf, block, block, 0, dev(far, x, y)).start()

    def enc_whole():
        got(c.ehalf, b.enc.at[pl.ds(0, NXY)])

    def sl_got():
        got(c.sl, b.a0.at[pl.ds(0, NXY - 1)])

    def times(w, a):
        return nn(a, weights[w][...].reshape(NZ * N, COLS))

    def pair(p):
        return jnp.concatenate([b.wo[2 * p], b.wo[2 * p + 1]], axis=1)

    def times_out_t(a):
        total = nt(a[:, : 2 * N], pair(0))
        for p in range(1, NZ // 2):
            total += nt(a[:, 2 * N * p : 2 * N * (p + 1)], pair(p))
        return total

    def dec_rows(buffer):
        return lambda yp: buffer[pl.ds(NX * yp, NX)].reshape(N, SL)

    def enc_group(yp):
        return b.enc[pl.ds(2 * NX * yp, 2 * NX)].reshape(N, SL)

    def project(step, rows_of, product, stage, landing, own, arrived=None):
        def one(k):
            yp = near(k)
            if arrived is not None:
                arrived(yp)
            stage[yp] = product(rows_of(yp)).astype(BF)
            copy(step, stage.at[yp], landing.at[y], 0, dev(s, x, yp)).start()

        if arrived is not None:
            arrived(y)
            own[...] = product(rows_of(y))
            each(1, NY, one)
        else:
            each(1, NY, one)
            own[...] = product(rows_of(y))

    def projected(step, landing, own):
        got(step, landing.at[pl.ds(0, NY - 1)])
        total = own[...]
        for k in range(1, NY):
            total += landing[(y + k) % NY].astype(F32)
        return total

    def head(value, h):
        return value[:, h * DK : (h + 1) * DK]

    def probabilities():
        for h in range(HEADS):
            scores = nt(head(b.q, h), head(b.k, h))
            scores = jnp.where(b.mask[...] > 0.5, scores, -1e30)
            top = jnp.max(scores, axis=-1, keepdims=True)
            e = jnp.exp(scores - top)
            b.prob[h] = e / jnp.sum(e, axis=-1, keepdims=True)

    def gather_y(step, buffer):
        def one(k):
            copy(step, buffer.at[y], buffer.at[y], y, dev(s, x, near(k))).start()

        each(1, NY, one)

    def attend():
        b.at[y] = jnp.concatenate(
            [nn(b.prob[h].astype(BF), head(b.v, h)) for h in range(HEADS)], axis=1
        ).astype(BF)
        gather_y(c.at, b.at)

    def query_gradient():
        grads = []
        for h in range(HEADS):
            prob = b.prob[h]
            prob_grad = nt(head(b.ag, h), head(b.v, h))
            score_grad = prob * (prob_grad - jnp.sum(prob_grad * prob, axis=-1, keepdims=True))
            b.sgt[h] = score_grad.T.astype(BF)
            grads.append(nn(score_grad.astype(BF), head(b.k, h)) * SCALE)
        low = jnp.concatenate(grads, axis=1).astype(BF)
        b.qg[y] = low
        gather_y(c.qg, b.qg)
        both = low.astype(F32) * b.q[...].astype(F32)
        lanes = both[:, :N]
        for f in range(1, COLS // N):
            lanes += both[:, f * N : (f + 1) * N]
        b.sp[...] = lanes.reshape(NX, ROWS, N)

    def key_value_gradients():
        for h in range(HEADS):
            b.pt[h] = b.prob[h].T.astype(BF)
        b.kg[y] = jnp.concatenate(
            [nn(b.sgt[h], head(b.q, h)) for h in range(HEADS)], axis=1
        ).astype(BF)
        gather_y(c.kg, b.kg)
        b.vg[y] = jnp.concatenate(
            [nn(b.pt[h], head(b.ag, h)) for h in range(HEADS)], axis=1
        ).astype(BF)
        gather_y(c.vg, b.vg)

    def update_rows(yp, stage):
        a = b.at[yp]
        for p in range(NZ // 2):
            part_out = nn(a, pair(p)).astype(BF).reshape(NX, ROWS, 2 * N)
            stage[pl.ds(NX * yp, NX), :, 2 * N * p : 2 * N * (p + 1)] = part_out

    def hidden_rows(yp, stage):
        a = b.qg[yp]
        for p in range(NZ // 2):
            block = b.wq[2 * p : 2 * p + 2].reshape(2 * N, COLS)
            part_out = nt(a, block).astype(BF).reshape(NX, ROWS, 2 * N)
            stage[pl.ds(NX * yp, NX), :, 2 * N * p : 2 * N * (p + 1)] = part_out

    def scatter_x(step, source_step, source, rows_into, stage, landing, sec, keep):
        def one(k):
            yp = near(k)

            @pl.when(k > 0)
            def _():
                got(source_step, source.at[yp], yp)

            rows_into(yp, stage)
            x_send(
                step,
                lambda xp: stage.at[NX * yp + xp],
                landing.at[NX * yp + x],
                sec,
                1 if keep else 0,
                yp,
            )
            if keep:
                landing[NX * yp + x] = stage[NX * yp + x]

        each(0, NY, one)

    def x_got(step, landing, yp, blocks):
        got(step, landing.at[pl.ds(NX * yp, blocks)], yp)

    def sum_x(landing, yp):
        total = landing[NX * yp].astype(F32)
        for i in range(1, NX):
            total += landing[NX * yp + i].astype(F32)
        return total

    def gather_x(yp):
        block = b.a1.at[NX * yp + x]
        x_send(c.a1, lambda xp: block, block, s, 1, yp)

    def a1_got(yp):
        x_got(c.a1, b.a1, yp, NX - 1)

    def across(tile):
        return jnp.concatenate([tile] * (SL // N), axis=1)

    def send_stat(step, landing, keep):
        x_send(step, lambda xp: b.sp.at[xp], landing.at[x], 0, 1 if keep else 0)
        if keep:
            landing[x] = b.sp[x]

    def share_stat(step, landing, result, step_out, blocks):
        got(step, landing.at[pl.ds(0, blocks)])
        lanes = landing[0] + landing[1] + landing[2] + landing[3]
        result[y] = jnp.broadcast_to(jnp.sum(lanes, axis=-1, keepdims=True), (ROWS, N))
        y_send(step_out, lambda i: result.at[y], result, 0, 1)

    def norm_gradient(yp, landing, gain_ref, rows, inv_ref, stat_ref, grad):
        u = sum_x(landing, yp) * gain_ref[0:1, :]
        inv = inv_ref[yp]
        coef = inv * inv * stat_ref[yp] * STAT
        wide_rows = rows[yp].astype(F32)
        return (grad[yp].astype(F32) + across(inv) * u - wide_rows * across(coef)).astype(BF)

    def memory_rows(yp, into):
        key = b.kg[yp]
        value = b.vg[yp]
        for p in range(NZ // 2):
            wk_block = b.wk[2 * p : 2 * p + 2].reshape(2 * N, COLS)
            wv_block = b.wv[2 * p : 2 * p + 2].reshape(2 * N, COLS)
            block = (nt(key, wk_block) + nt(value, wv_block)).reshape(2 * NX, EROWS, 2 * N)
            into(slice(2 * N * p, 2 * N * (p + 1)), block)

    def kv_got(k):
        yp = near(k)

        @pl.when(k > 0)
        def _():
            got(c.kg, b.kg.at[yp], yp)
            got(c.vg, b.vg.at[yp], yp)

        return yp

    @pl.when(s == 0)
    def _():
        ring_send(Q, 0)
        ring_send(K, 0)
        ring_send(V, 0)
        enc_start()
        sl_start()
        ring_next(1, Q, K, V)
        ring_send(O, 0)
        small_start()
        y_send(c.inv0, lambda i: b.inv0s, b.inv0, 0, 1)
        ring_next(2, Q, K, V)
        ring_next(1, O)
        enc_half()
        ring_next(3, Q, K, V)
        ring_next(2, O)
        sl_got()
        ring_got(Q, 3)
        project(c.pq, dec_rows(b.a0), lambda a: times(Q, a), b.s_q, b.r_q, b.own_q)
        ring_next(3, O)
        pl.semaphore_signal(go, inc=1, device_id=dev(1, x, y), device_id_type=MESH)
        enc_whole()
        ring_got(K, 3)
        project(c.pk, enc_group, lambda a: times(K, a), b.s_k, b.r_k, b.own_k)
        ring_got(V, 3)
        project(c.pv, enc_group, lambda a: times(V, a), b.s_v, b.r_v, b.own_v)
        b.q[...] = (projected(c.pq, b.r_q, b.own_q) * SCALE).astype(BF)
        b.k[...] = projected(c.pk, b.r_k, b.own_k).astype(BF)
        probabilities()
        b.v[...] = projected(c.pv, b.r_v, b.own_v).astype(BF)
        attend()
        ring_got(O, 3)
        scatter_x(c.xa, c.at, b.at, update_rows, b.sxa, b.rxa, 1, False)

        got(c.gain, b.gain_far)
        got(c.c0, b.c0)
        got(c.dsl, b.x0.at[pl.ds(0, NY - 1)])
        got(c.inv0, b.inv0.at[pl.ds(0, NY - 1)])
        got(c.x1, b.x1)
        got(c.inv1, b.inv1)
        share_stat(c.spr1, b.spr1, b.sall1, c.sall1, NX)

        def grad_one(k):
            yp = near(k)
            x_got(c.xa, b.rxa, yp, NX)

            @pl.when(k == 1)
            def _():
                got(c.sall1, b.sall1.at[pl.ds(0, NY - 1)])

            g = norm_gradient(yp, b.rxa, b.gain_far, b.x1, b.inv1, b.sall1, b.c0)
            b.t1[yp] = g
            b.a1[NX * yp + x] = g
            gather_x(yp)

        each(0, NY, grad_one)
        y_send(c.sgr, lambda i: b.t1.at[i], b.sgr, 1, 0)

        project(c.pag, dec_rows(b.a1), times_out_t, b.s_ag, b.r_ag, b.own_ag, a1_got)
        b.ag[...] = projected(c.pag, b.r_ag, b.own_ag).astype(BF)
        query_gradient()
        send_stat(c.spr0, b.spr0, True)
        key_value_gradients()
        scatter_x(c.xb, c.qg, b.qg, hidden_rows, b.sxb, b.rxb, 0, True)
        share_stat(c.spr0, b.spr0, b.sall0, c.sall0, NX - 1)

        def memory_zero(k):
            yp = kv_got(k)
            far_rows = b.mgc.at[pl.ds(2 * NX * yp, 2 * NX)]
            got(c.mgc, far_rows, yp)

            def into(lanes, block):
                total = block + far_rows[:, :, lanes].astype(F32)
                b.mgs[pl.ds(2 * NX * yp, 2 * NX), :, lanes] = total.astype(BF)

            memory_rows(yp, into)
            for sec in range(2):
                x_send(
                    c.rm,
                    lambda xp, sec=sec: b.mgs.at[(2 * yp + sec) * NX + xp],
                    b.rm.at[NX * yp + x],
                    sec,
                    1 - sec,
                    yp,
                )
            b.rm[NX * yp + x] = b.mgs[2 * NX * yp + x]

        each(0, NY, memory_zero)

        def grad_zero(k):
            yp = near(k)
            x_got(c.xb, b.rxb, yp, NX - 1)

            @pl.when(k == 1)
            def _():
                got(c.sall0, b.sall0.at[pl.ds(0, NY - 1)])

            b.t2[yp] = norm_gradient(yp, b.rxb, b.gain, b.x0, b.inv0, b.sall0, b.t1)

            @pl.when(k > 0)
            def _():
                copy(c.sgr0, b.t2.at[yp], b.sgr.at[y], 0, dev(0, x, yp)).start()

        each(0, NY, grad_zero)
        b.sgr[y] = b.t2[y]

    @pl.when(s == 1)
    def _():
        enc_start()
        small_start()
        enc_half()
        got(c.dsl, b.x0.at[pl.ds(0, NY - 1)])
        got(c.gain, b.gain_far)
        enc_whole()
        pl.semaphore_wait(go, 1)
        ring_send(K, 0)
        ring_send(V, 0)
        ring_send(O, 0)
        sl_start()
        ring_next(1, K, V, O)
        ring_send(Q, 0)
        ring_next(2, K, V, O)
        ring_next(1, Q)
        ring_next(3, K, V, O)
        ring_next(2, Q)
        ring_got(K, 3)
        project(c.pk, enc_group, lambda a: times(K, a), b.s_k, b.r_k, b.own_k)
        ring_next(3, Q)
        ring_got(V, 3)
        project(c.pv, enc_group, lambda a: times(V, a), b.s_v, b.r_v, b.own_v)
        sl_got()
        for yp in range(NY):
            copy(c.c0, b.a0.at[NX * yp + x], b.c0.at[yp], 0, dev(0, x, y)).start()
        ring_got(O, 3)
        project(c.pag, dec_rows(b.a0), times_out_t, b.s_ag, b.r_ag, b.own_ag)
        b.k[...] = projected(c.pk, b.r_k, b.own_k).astype(BF)
        b.v[...] = projected(c.pv, b.r_v, b.own_v).astype(BF)
        b.ag[...] = projected(c.pag, b.r_ag, b.own_ag).astype(BF)
        ring_got(Q, 3)

        def stream_one(k):
            yp = near(k)
            x_got(c.xa, b.rxa, yp, NX)
            rows = (b.x0[yp].astype(F32) + sum_x(b.rxa, yp)).astype(BF)
            b.x1[yp] = rows
            rows = rows.astype(F32)
            b.a1[NX * yp + x] = (rows * b.gain[0:1, :]).astype(BF)
            gather_x(yp)
            squares = rows * rows
            lanes = squares[:, :N]
            for f in range(1, SL // N):
                lanes += squares[:, f * N : (f + 1) * N]
            b.ss[y, yp] = lanes

        each(0, NY, stream_one)
        y_send(c.ss, lambda i: b.ss.at[y], b.ss, 1, 1)
        copy(c.x1, b.x1, b.x1, 0, dev(0, x, y)).start()
        y_send(c.por, lambda i: b.x1.at[i], b.por, 0, 0)
        got(c.ss, b.ss.at[pl.ds(0, NY - 1)])

        def inverse_one(yp):
            lanes = b.ss[0, yp] + b.ss[1, yp] + b.ss[2, yp] + b.ss[3, yp]
            inv = lax.rsqrt(jnp.sum(lanes, axis=-1, keepdims=True) * (1.0 / D) + EPS)
            b.inv1[yp] = jnp.broadcast_to(inv, (ROWS, N))

        each(0, NY, inverse_one)
        b.invx[x] = b.inv1[y]
        x_send(c.invx, lambda xp: b.inv1.at[y], b.invx.at[x], 1, 1)
        copy(c.inv1, b.inv1, b.inv1, 0, dev(0, x, y)).start()
        project(c.pq, dec_rows(b.a1), lambda a: times(Q, a), b.s_q, b.r_q, b.own_q, a1_got)
        got(c.invx, b.invx.at[pl.ds(0, NX - 1)])
        row_scale = b.invx[...].reshape(N, N) * SCALE
        row_scale = jnp.concatenate([row_scale] * (COLS // N), axis=1)
        b.q[...] = (projected(c.pq, b.r_q, b.own_q) * row_scale).astype(BF)
        probabilities()
        query_gradient()
        send_stat(c.spr1, b.spr1, False)
        scatter_x(c.xa, c.qg, b.qg, hidden_rows, b.sxa, b.rxa, 0, False)

        key_value_gradients()

        def memory_one(k):
            yp = kv_got(k)

            def into(lanes, block):
                b.mgs[pl.ds(2 * NX * yp, 2 * NX), :, lanes] = block.astype(BF)

            memory_rows(yp, into)
            rows = pl.ds(2 * NX * yp, 2 * NX)
            copy(c.mgc, b.mgs.at[rows], b.mgc.at[rows], yp, dev(0, x, y)).start()

        each(0, NY, memory_one)
        attend()
        scatter_x(c.xb, c.at, b.at, update_rows, b.sxb, b.rxb, 1, True)

        def output_one(k):
            yp = near(k)
            x_got(c.xb, b.rxb, yp, NX - 1)
            b.t2[yp] = (b.x1[yp].astype(F32) + sum_x(b.rxb, yp)).astype(BF)

        each(0, NY, output_one)
        y_send(c.por1, lambda i: b.t2.at[i], b.por, 1, 1)
        b.por[y] = b.t2[y]

    store_p = local(b.por, out_p, 10)
    store_s = local(b.sgr, out_s, 11)
    store_m = local(b.mo, out_m, 12)

    @pl.when(s == 0)
    def _():
        got(c.por, b.por)

    @pl.when(s == 1)
    def _():
        got(c.por1, b.por.at[pl.ds(0, NY - 1)])
        got(c.sgr, b.sgr)
        store_s.start()

    store_p.start()

    def memory_sum(k):
        yp = near(k)

        @pl.when(s == 0)
        def _():
            x_got(c.rm, b.rm, yp, NX - 1)

        @pl.when(s == 1)
        def _():
            x_got(c.rm, b.rm, yp, NX)

        b.mos[yp] = sum_x(b.rm, yp).astype(BF)

        @pl.when(k > 0)
        def _():
            copy(c.mo, b.mos.at[yp], b.mo.at[y], 0, dev(s, x, yp)).start()

    each(0, NY, memory_sum)
    b.mo[y] = b.mos[y]

    @pl.when(s == 0)
    def _():
        got(c.sgr0, b.sgr.at[pl.ds(0, NY - 1)])
        store_s.start()

    got(c.mo, b.mo.at[pl.ds(0, NY - 1)])
    store_m.start()

    three = pl.ds(0, NY - 1)
    for w in range(4):
        sent(rings[w], weights[w].at[pl.ds(0, NZ - 1)])
    sent(c.sl, b.a0.at[pl.ds(0, NXY - 1)])
    sent(c.enc, b.enc.at[pl.ds(0, NXY - 1)])
    sent(c.ehalf, b.enc.at[pl.ds(0, NXY)])
    sent(c.dsl, b.dsl.at[three])
    sent(c.gain, b.gain)
    for step in (c.pq, c.pk, c.pv, c.pag, c.at, c.qg, c.kg, c.vg):
        sent(step, b.s_q.at[three])
    sent(c.a1, b.a1.at[pl.ds(0, NXY - NY)])
    sent(c.xa, b.sxa)
    sent(c.xb, b.sxb.at[pl.ds(0, NXY - NY)])
    sent(c.mo, b.mos.at[three])

    @pl.when(s == 0)
    def _():
        sent(c.inv0, b.inv0.at[three])
        sent(c.sall1, b.sall1.at[three])
        sent(c.sall0, b.sall0.at[three])
        sent(c.spr0, b.sp.at[three])
        sent(c.sgr, b.t1)
        sent(c.sgr0, b.t2.at[three])
        sent(c.rm, b.mgs.at[pl.ds(0, 2 * NXY - NY)])

    @pl.when(s == 1)
    def _():
        sent(c.c0, b.c0)
        sent(c.x1, b.x1)
        sent(c.inv1, b.inv1)
        sent(c.mgc, b.mgs)
        sent(c.por, b.x1)
        sent(c.por1, b.t2.at[three])
        sent(c.ss, b.ss.at[three])
        sent(c.invx, b.invx.at[three])
        sent(c.spr1, b.sp)

    store_p.wait()
    store_s.wait()
    store_m.wait()


def assemble(phase, stream, memory, out_p, out_s, out_m):
    for source, out in ((phase, out_p), (stream, out_s), (memory, out_m)):
        for yp in range(NY):
            value = source[yp]
            for f in range(NZ):
                at = (NY * f + yp) * N
                out[:, at : at + N] = value[:, f * N : (f + 1) * N].astype(out.dtype)


def body(*args):
    dec, enc, dseg, eseg, gain, wq, wk, wv, wo, cot = args
    parts = pl.pallas_call(
        kernel,
        out_shape=(
            jax.ShapeDtypeStruct((NY, ROWS, SL), BF),
            jax.ShapeDtypeStruct((NY, ROWS, SL), BF),
            jax.ShapeDtypeStruct((NY, EROWS, SL), BF),
        ),
        in_specs=[pl.BlockSpec(memory_space=pl.ANY)] * 10,
        out_specs=(pl.BlockSpec(memory_space=pl.ANY),) * 3,
        scratch_shapes=list(BUFFERS.values())
        + [pltpu.SemaphoreType.DMA(shape) for shape in COPIES.values()]
        + [
            pltpu.SemaphoreType.DMA((len(COPIES),)),
            pltpu.SemaphoreType.DMA((LOCAL,)),
            pltpu.SemaphoreType.REGULAR,
        ],
        compiler_params=pltpu.CompilerParams(
            collective_id=0, has_side_effects=True, vmem_limit_bytes=56 * 2**20
        ),
        cost_estimate=pl.CostEstimate(
            flops=16 * 2**30, bytes_accessed=4 * 2**20, transcendentals=2**16
        ),
        name="decoder_phases",
    )(dec[0], enc[0], dseg, eseg, gain, wq[0], wk[0], wv[0], wo[0], cot[0])
    phase, stream, memory = pl.pallas_call(
        assemble,
        out_shape=(
            jax.ShapeDtypeStruct((ROWS, D), BF),
            jax.ShapeDtypeStruct((ROWS, D), BF),
            jax.ShapeDtypeStruct((EROWS, D), F32),
        ),
        in_specs=[pl.BlockSpec(memory_space=pltpu.VMEM)] * 3,
        out_specs=(pl.BlockSpec(memory_space=pltpu.VMEM),) * 3,
        name="assemble",
    )(*parts)
    return phase[None, None], stream[None, None], memory[None]


def solution(mesh):
    in_specs = (
        P("dp", "mp", None),
        P("dp", ("section", "mp"), None),
        P("dp", None),
        P("dp", None),
        P("section", None),
        P("section", "dp", "mp"),
        P("section", "dp", "mp"),
        P("section", "dp", "mp"),
        P("section", "mp", "dp"),
        P("dp", "mp", None),
    )
    out_specs = (
        P("section", "dp", "mp", None),
        P("section", "dp", "mp", None),
        P("dp", ("section", "mp"), None),
    )
    return jax.shard_map(body, mesh=mesh, in_specs=in_specs, out_specs=out_specs, check_vma=False)
```

```python
from types import SimpleNamespace

import jax
import jax.numpy as jnp
from jax import lax
from jax.experimental import pallas as pl
from jax.experimental.pallas import tpu as pltpu
from jax.sharding import PartitionSpec as P

MESH = pl.DeviceIdType.MESH
BF = jnp.bfloat16
F32 = jnp.float32

NX, NY, NZ = 4, 4, 8
NXY = NX * NY
D = 4096
DK = 256
COLS = 512
HEADS = COLS // DK
ROWS = 32
EROWS = 16
SL = D // NY
N = 128
EPS = 1e-06
SCALE = DK ** (-0.5)
STAT = 1.0 / (D * SCALE)
Q, K, V, O = range(4)
ORDER = (0, 1, 3, 2)


def vm(*shape, dtype=BF):
    return pltpu.VMEM(shape, dtype)


BUFFERS = dict(
    wq=vm(NZ, N, COLS),
    wk=vm(NZ, N, COLS),
    wv=vm(NZ, N, COLS),
    wo=vm(NZ, COLS, N),
    dec=vm(ROWS, D),
    enc_in=vm(EROWS, D),
    cot=vm(ROWS, D),
    gain_in=vm(1, D, dtype=F32),
    dseg=vm(1, N, dtype=jnp.int32),
    eseg=vm(1, N, dtype=jnp.int32),
    esl=vm(NY, EROWS, SL),
    enc=vm(2 * NXY, EROWS, SL),
    sl=vm(NY, ROWS, SL),
    a0=vm(NXY, ROWS, SL),
    a1=vm(NXY, ROWS, SL),
    dsl=vm(NY, ROWS, SL),
    x0=vm(NY, ROWS, SL),
    c0=vm(NY, ROWS, SL),
    x1=vm(NY, ROWS, SL),
    t1=vm(NY, ROWS, SL),
    t2=vm(NY, ROWS, SL),
    inv0s=vm(ROWS, N, dtype=F32),
    inv0=vm(NY, ROWS, N, dtype=F32),
    inv1=vm(NY, ROWS, N, dtype=F32),
    invx=vm(NX, ROWS, N, dtype=F32),
    gain=vm(8, SL, dtype=F32),
    gain_far=vm(8, SL, dtype=F32),
    mask=vm(N, N, dtype=F32),
    prob=vm(HEADS, N, N, dtype=F32),
    pg=vm(HEADS, N, N, dtype=F32),
    sgt=vm(HEADS, N, N),
    pt=vm(HEADS, N, N),
    q=vm(N, COLS),
    k=vm(N, COLS),
    v=vm(N, COLS),
    ag=vm(N, COLS),
    own_q=vm(N, COLS, dtype=F32),
    own_k=vm(N, COLS, dtype=F32),
    own_v=vm(N, COLS, dtype=F32),
    own_ag=vm(N, COLS, dtype=F32),
    s_q=vm(NY, N, COLS),
    s_k=vm(NY, N, COLS),
    s_v=vm(NY, N, COLS),
    s_ag=vm(NY, N, COLS),
    r_q=vm(NY, N, COLS),
    r_k=vm(NY, N, COLS),
    r_v=vm(NY, N, COLS),
    r_ag=vm(NY, N, COLS),
    at=vm(NY, N, COLS),
    qg=vm(NY, N, COLS),
    kg=vm(NY, N, COLS),
    vg=vm(NY, N, COLS),
    sxa=vm(NXY, ROWS, SL),
    sxb=vm(NXY, ROWS, SL),
    rxa=vm(NXY, ROWS, SL),
    rxb=vm(NXY, ROWS, SL),
    ss=vm(NY, NY, ROWS, N, dtype=F32),
    sp=vm(NX, ROWS, N, dtype=F32),
    spr1=vm(NX, ROWS, N, dtype=F32),
    spr0=vm(NX, ROWS, N, dtype=F32),
    sall1=vm(NY, ROWS, N, dtype=F32),
    sall0=vm(NY, ROWS, N, dtype=F32),
    por=vm(NY, ROWS, SL),
    sgr=vm(NY, ROWS, SL),
    mgs=vm(2 * NXY, EROWS, SL),
    mgc=vm(2 * NXY, EROWS, SL),
    rm=vm(NXY, EROWS, SL),
    mos=vm(NY, EROWS, SL),
    mo=vm(NY, EROWS, SL),
)

COPIES = dict(
    ring_q=(2, 4),
    ring_k=(2, 4),
    ring_v=(2, 4),
    ring_o=(2, 4),
    enc=(1,),
    sl=(1,),
    dsl=(1,),
    inv0=(1,),
    gain=(1,),
    ehalf=(1,),
    c0=(1,),
    pq=(1,),
    pk=(1,),
    pv=(1,),
    pag=(1,),
    at=(NY,),
    qg=(NY,),
    kg=(NY,),
    vg=(NY,),
    xa=(NY,),
    xb=(NY,),
    a1=(NY,),
    ss=(1,),
    invx=(1,),
    inv1=(1,),
    x1=(1,),
    spr1=(1,),
    spr0=(1,),
    sall1=(1,),
    sall0=(1,),
    por=(1,),
    por1=(1,),
    sgr=(1,),
    sgr0=(1,),
    mgc=(NY,),
    rm=(NY,),
    mo=(1,),
)
LOCAL = 13


def nn(a, b):
    return jnp.dot(a, b, preferred_element_type=F32)


def nt(a, b):
    return lax.dot_general(a, b, (((1,), (1,)), ((), ())), preferred_element_type=F32)


def kernel(*refs):
    dec, enc_in, dseg, eseg, gain_in, wq_in, wk_in, wv_in, wo_in, cot = refs[:10]
    out_p, out_s, out_m = refs[10:13]
    scratch = refs[13:]
    b = SimpleNamespace(**dict(zip(BUFFERS, scratch)))
    rest = scratch[len(BUFFERS) :]
    send_sems, local_sems, go = rest[len(COPIES) :]
    c = SimpleNamespace(**{n: (r, i) for i, (n, r) in enumerate(zip(COPIES, rest))})

    s = lax.axis_index("section")
    x = lax.axis_index("mp")
    dp = lax.axis_index("dp")
    y = dp % NY
    z = dp // NY
    far = 1 - s

    def dev(sec, xx, yy, zz=None):
        return {"section": sec, "mp": xx, "dp": (z if zz is None else zz) * NY + yy}

    here = dev(s, x, y)

    def copy(step, src, dst, at, device):
        return pltpu.make_async_remote_copy(
            src_ref=src,
            dst_ref=dst,
            send_sem=send_sems.at[step[1]],
            recv_sem=step[0].at[at],
            device_id=device,
            device_id_type=MESH,
        )

    def got(step, ref, at=0):
        copy(step, ref, ref, at, here).wait_recv()

    def sent(step, ref):
        first = (0,) * len(step[0].shape)
        copy(step, ref, ref, first, here).wait_send()

    def each(lo, hi, body):
        lax.fori_loop(lo, hi, lambda i, carry: (body(i), carry)[1], 0)

    def by_distance(i):
        return i + (i // 2) * (5 - 2 * i)

    def near(k):
        return (y + by_distance(k)) % NY

    def y_send(step, src_of, dst, sec, lo, at=None):
        def one(k):
            yp = (y + k) % NY
            copy(step, src_of(yp), dst.at[y], 0 if at is None else at, dev(sec, x, yp)).start()

        each(lo, NY, one)

    def x_send(step, src_of, dst, sec, lo, at=0):
        def one(k):
            xp = (x + k) % NX
            copy(step, src_of(xp), dst, at, dev(sec, xp, y)).start()

        each(lo, NX, one)

    weights = (b.wq, b.wk, b.wv, b.wo)
    rings = (c.ring_q, c.ring_k, c.ring_v, c.ring_o)

    def part(w, slot, step, way):
        ref = weights[w]
        if step < 3:
            return ref.at[slot]
        half = ref.shape[1] // 2
        return ref.at[slot, pl.ds(way * half, half)]

    def ring_send(w, step):
        for way in range(2):
            slot = (z + NZ - step) % NZ if way == 0 else (z + step) % NZ
            to = (z + 1) % NZ if way == 0 else (z + NZ - 1) % NZ
            ref = part(w, slot, step, way)
            copy(rings[w], ref, ref, (way, step), dev(s, x, y, to)).start()

    def ring_got(w, step):
        for way in range(2):
            slot = (z + NZ - 1 - step) % NZ if way == 0 else (z + 1 + step) % NZ
            got(rings[w], part(w, slot, step, way), (way, step))

    def ring_next(step, *ws):
        for w in ws:
            ring_got(w, step - 1)
            ring_send(w, step)

    barrier = pltpu.get_barrier_semaphore()

    def hello(device):
        pl.semaphore_signal(barrier, inc=1, device_id=device, device_id_type=MESH)

    def hello_xy(k):
        t = (NX * y + x + k) % NXY
        hello(dev(s, t % NX, t // NX))

    each(1, NXY, hello_xy)
    hello(dev(s, x, y, (z + 1) % NZ))
    hello(dev(s, x, y, (z + NZ - 1) % NZ))
    each(0, NX, lambda k: hello(dev(far, (x + k) % NX, y)))
    each(1, NY, lambda k: hello(dev(far, x, (y + k) % NY)))

    def local(src, dst, i):
        return pltpu.make_async_copy(src, dst, local_sems.at[i])

    loads = [
        local(src, dst, i)
        for i, (src, dst) in enumerate(
            (
                (dec, b.dec),
                (gain_in, b.gain_in),
                (enc_in, b.enc_in),
                (dseg, b.dseg),
                (eseg, b.eseg),
                (cot, b.cot),
                (wq_in, b.wq.at[z]),
                (wk_in, b.wk.at[z]),
                (wv_in, b.wv.at[z]),
                (wo_in, b.wo.at[z]),
            )
        )
    ]
    for load in loads:
        load.start()
    for load in loads:
        load.wait()

    def pick(value, yp):
        return jnp.concatenate(
            [value[:, (NY * f + yp) * N : (NY * f + yp + 1) * N] for f in range(NZ)], axis=1
        )

    rows_in = b.dec[...]
    enc_rows = b.enc_in[...]

    @pl.when(s == 0)
    def _():
        wide = rows_in.astype(F32)
        inverse = lax.rsqrt(jnp.mean(wide * wide, axis=-1, keepdims=True) + EPS)
        inv_tile = jnp.broadcast_to(inverse, (ROWS, N))
        b.inv0s[...] = inv_tile
        b.inv0[y] = inv_tile
        hidden = (wide * inverse * b.gain_in[...]).astype(BF)
        for yp in range(NY):
            b.sl[yp] = pick(hidden, yp)

    @pl.when(s == 1)
    def _():
        value = b.cot[...]
        for yp in range(NY):
            b.sl[yp] = pick(value, yp)

    for yp in range(NY):
        b.dsl[yp] = pick(rows_in, yp)
        b.esl[yp] = pick(enc_rows, yp)
    b.a0[NX * y + x] = b.sl[y]
    b.x0[y] = b.dsl[y]
    b.enc[(2 * y + s) * NX + x] = b.esl[y]
    for f in range(NZ):
        own_gain = b.gain_in[:, pl.ds(pl.multiple_of((NY * f + y) * N, N), N)]
        b.gain[:, f * N : (f + 1) * N] = jnp.broadcast_to(own_gain, (8, N))
    dec_ids = jnp.broadcast_to(b.dseg[...].astype(F32), (N, N)).T
    enc_ids = jnp.broadcast_to(b.eseg[...].astype(F32), (N, N))
    b.mask[...] = jnp.where(dec_ids == enc_ids, 1.0, 0.0)

    pl.semaphore_wait(barrier, NXY - 1 + 2 + NX + NY - 1)

    def xy_start(step, src, dst):
        def one(k):
            t = (NX * y + x + k) % NXY
            copy(step, src.at[t // NX], dst, 0, dev(s, t % NX, t // NX)).start()

        each(1, NXY, one)

    def enc_start():
        xy_start(c.enc, b.esl, b.enc.at[(2 * y + s) * NX + x])

    def sl_start():
        xy_start(c.sl, b.sl, b.a0.at[NX * y + x])

    def small_start():
        copy(c.gain, b.gain, b.gain_far, 0, dev(far, x, y)).start()
        y_send(c.dsl, lambda i: b.dsl.at[i], b.x0, s, 1)

    def enc_half():
        got(c.enc, b.enc.at[pl.ds(0, NXY - 1)])
        for yp in range(NY):
            block = b.enc.at[pl.ds((2 * yp + s) * NX, NX)]
            copy(c.ehalf, block, block, 0, dev(far, x, y)).start()

    def enc_whole():
        got(c.ehalf, b.enc.at[pl.ds(0, NXY)])

    def sl_got():
        got(c.sl, b.a0.at[pl.ds(0, NXY - 1)])

    def times(w, a):
        return nn(a, weights[w][...].reshape(NZ * N, COLS))

    def pair(p):
        return jnp.concatenate([b.wo[2 * p], b.wo[2 * p + 1]], axis=1)

    def times_out_t(a):
        total = nt(a[:, : 2 * N], pair(0))
        for p in range(1, NZ // 2):
            total += nt(a[:, 2 * N * p : 2 * N * (p + 1)], pair(p))
        return total

    def dec_rows(buffer):
        return lambda yp: buffer[pl.ds(NX * yp, NX)].reshape(N, SL)

    def enc_group(yp):
        return b.enc[pl.ds(2 * NX * yp, 2 * NX)].reshape(N, SL)

    def project(step, rows_of, product, stage, landing, own, arrived=None):
        def one(k):
            yp = near(k)
            if arrived is not None:
                arrived(yp)
            stage[yp] = product(rows_of(yp)).astype(BF)
            copy(step, stage.at[yp], landing.at[y], 0, dev(s, x, yp)).start()

        if arrived is not None:
            arrived(y)
            own[...] = product(rows_of(y))
            each(1, NY, one)
        else:
            each(1, NY, one)
            own[...] = product(rows_of(y))

    def projected(step, landing, own):
        got(step, landing.at[pl.ds(0, NY - 1)])
        total = own[...]
        for k in range(1, NY):
            total += landing[(y + k) % NY].astype(F32)
        return total

    def head(value, h):
        return value[:, h * DK : (h + 1) * DK]

    def probabilities():
        for h in range(HEADS):
            scores = nt(head(b.q, h), head(b.k, h))
            scores = jnp.where(b.mask[...] > 0.5, scores, -1e30)
            top = jnp.max(scores, axis=-1, keepdims=True)
            e = jnp.exp(scores - top)
            b.prob[h] = e / jnp.sum(e, axis=-1, keepdims=True)

    def gather_y(step, buffer):
        def one(k):
            copy(step, buffer.at[y], buffer.at[y], y, dev(s, x, near(k))).start()

        each(1, NY, one)

    def attend():
        b.at[y] = jnp.concatenate(
            [nn(b.prob[h].astype(BF), head(b.v, h)) for h in range(HEADS)], axis=1
        ).astype(BF)
        gather_y(c.at, b.at)

    def probability_gradient():
        for h in range(HEADS):
            b.pg[h] = nt(head(b.ag, h), head(b.v, h))

    def query_gradient():
        grads = []
        for h in range(HEADS):
            prob = b.prob[h]
            prob_grad = b.pg[h]
            score_grad = prob * (prob_grad - jnp.sum(prob_grad * prob, axis=-1, keepdims=True))
            b.sgt[h] = score_grad.T.astype(BF)
            grads.append(nn(score_grad.astype(BF), head(b.k, h)) * SCALE)
        low = jnp.concatenate(grads, axis=1).astype(BF)
        b.qg[y] = low
        gather_y(c.qg, b.qg)
        both = low.astype(F32) * b.q[...].astype(F32)
        lanes = both[:, :N]
        for f in range(1, COLS // N):
            lanes += both[:, f * N : (f + 1) * N]
        b.sp[...] = lanes.reshape(NX, ROWS, N)

    def key_value_gradients():
        for h in range(HEADS):
            b.pt[h] = b.prob[h].T.astype(BF)
        b.kg[y] = jnp.concatenate(
            [nn(b.sgt[h], head(b.q, h)) for h in range(HEADS)], axis=1
        ).astype(BF)
        gather_y(c.kg, b.kg)
        b.vg[y] = jnp.concatenate(
            [nn(b.pt[h], head(b.ag, h)) for h in range(HEADS)], axis=1
        ).astype(BF)
        gather_y(c.vg, b.vg)

    def update_rows(yp, stage):
        a = b.at[yp]
        for p in range(NZ // 2):
            part_out = nn(a, pair(p)).astype(BF).reshape(NX, ROWS, 2 * N)
            stage[pl.ds(NX * yp, NX), :, 2 * N * p : 2 * N * (p + 1)] = part_out

    def hidden_rows(yp, stage):
        a = b.qg[yp]
        for p in range(NZ // 2):
            block = b.wq[2 * p : 2 * p + 2].reshape(2 * N, COLS)
            part_out = nt(a, block).astype(BF).reshape(NX, ROWS, 2 * N)
            stage[pl.ds(NX * yp, NX), :, 2 * N * p : 2 * N * (p + 1)] = part_out

    def scatter_x(step, source_step, source, rows_into, stage, landing, sec, keep, then=None):
        def one(k):
            yp = near(k)

            if not isinstance(k, int):

                @pl.when(k > 0)
                def _():
                    got(source_step, source.at[yp], yp)

            rows_into(yp, stage)
            x_send(
                step,
                lambda xp: stage.at[NX * yp + xp],
                landing.at[NX * yp + x],
                sec,
                1 if keep else 0,
                yp,
            )
            if keep:
                landing[NX * yp + x] = stage[NX * yp + x]

        if then is None:
            each(0, NY, one)
        else:
            one(0)
            then()
            each(1, NY, one)

    def x_got(step, landing, yp, blocks):
        got(step, landing.at[pl.ds(NX * yp, blocks)], yp)

    def sum_x(landing, yp):
        total = landing[NX * yp].astype(F32)
        for i in range(1, NX):
            total += landing[NX * yp + i].astype(F32)
        return total

    def gather_x(yp):
        block = b.a1.at[NX * yp + x]
        x_send(c.a1, lambda xp: block, block, s, 1, yp)

    def a1_got(yp):
        x_got(c.a1, b.a1, yp, NX - 1)

    def across(tile):
        return jnp.concatenate([tile] * (SL // N), axis=1)

    def send_stat(step, landing, keep):
        x_send(step, lambda xp: b.sp.at[xp], landing.at[x], 0, 1 if keep else 0)
        if keep:
            landing[x] = b.sp[x]

    def share_stat(step, landing, result, step_out, blocks):
        got(step, landing.at[pl.ds(0, blocks)])
        lanes = landing[0] + landing[1] + landing[2] + landing[3]
        result[y] = jnp.broadcast_to(jnp.sum(lanes, axis=-1, keepdims=True), (ROWS, N))
        y_send(step_out, lambda i: result.at[y], result, 0, 1)

    def norm_gradient(yp, landing, gain_ref, rows, inv_ref, stat_ref, grad):
        u = sum_x(landing, yp) * gain_ref[0:1, :]
        inv = inv_ref[yp]
        coef = inv * inv * stat_ref[yp] * STAT
        wide_rows = rows[yp].astype(F32)
        return (grad[yp].astype(F32) + across(inv) * u - wide_rows * across(coef)).astype(BF)

    def memory_rows(yp, into):
        key = b.kg[yp]
        value = b.vg[yp]
        for p in range(NZ // 2):
            wk_block = b.wk[2 * p : 2 * p + 2].reshape(2 * N, COLS)
            wv_block = b.wv[2 * p : 2 * p + 2].reshape(2 * N, COLS)
            block = (nt(key, wk_block) + nt(value, wv_block)).reshape(2 * NX, EROWS, 2 * N)
            into(slice(2 * N * p, 2 * N * (p + 1)), block)

    def kv_got(k):
        yp = near(k)

        @pl.when(k > 0)
        def _():
            got(c.kg, b.kg.at[yp], yp)
            got(c.vg, b.vg.at[yp], yp)

        return yp

    @pl.when(s == 0)
    def _():
        for w in (Q, K, V):
            ring_send(w, 0)
        enc_start()
        sl_start()
        ring_next(1, Q, K, V)
        small_start()
        y_send(c.inv0, lambda i: b.inv0s, b.inv0, 0, 1)
        ring_next(2, Q, K, V)
        ring_send(O, 0)
        enc_half()
        ring_next(3, Q, K, V)
        pl.semaphore_signal(go, inc=1, device_id=dev(1, x, y), device_id_type=MESH)
        ring_next(1, O)
        sl_got()
        ring_got(Q, 3)
        project(c.pq, dec_rows(b.a0), lambda a: times(Q, a), b.s_q, b.r_q, b.own_q)
        ring_next(2, O)
        enc_whole()
        ring_got(K, 3)
        project(c.pk, enc_group, lambda a: times(K, a), b.s_k, b.r_k, b.own_k)
        ring_next(3, O)
        ring_got(V, 3)
        project(c.pv, enc_group, lambda a: times(V, a), b.s_v, b.r_v, b.own_v)
        b.q[...] = (projected(c.pq, b.r_q, b.own_q) * SCALE).astype(BF)
        b.k[...] = projected(c.pk, b.r_k, b.own_k).astype(BF)
        probabilities()
        b.v[...] = projected(c.pv, b.r_v, b.own_v).astype(BF)
        attend()
        ring_got(O, 3)
        scatter_x(c.xa, c.at, b.at, update_rows, b.sxa, b.rxa, 1, False)

        got(c.gain, b.gain_far)
        got(c.c0, b.c0)
        got(c.dsl, b.x0.at[pl.ds(0, NY - 1)])
        got(c.inv0, b.inv0.at[pl.ds(0, NY - 1)])
        got(c.x1, b.x1)
        got(c.inv1, b.inv1)
        share_stat(c.spr1, b.spr1, b.sall1, c.sall1, NX)

        def grad_one(k):
            yp = near(k)
            x_got(c.xa, b.rxa, yp, NX)

            @pl.when(k == 1)
            def _():
                got(c.sall1, b.sall1.at[pl.ds(0, NY - 1)])

            g = norm_gradient(yp, b.rxa, b.gain_far, b.x1, b.inv1, b.sall1, b.c0)
            b.t1[yp] = g
            b.a1[NX * yp + x] = g
            gather_x(yp)

        each(0, NY, grad_one)
        y_send(c.sgr, lambda i: b.t1.at[i], b.sgr, 1, 0)

        project(c.pag, dec_rows(b.a1), times_out_t, b.s_ag, b.r_ag, b.own_ag, a1_got)
        b.ag[...] = projected(c.pag, b.r_ag, b.own_ag).astype(BF)
        probability_gradient()
        query_gradient()
        send_stat(c.spr0, b.spr0, True)
        scatter_x(c.xb, c.qg, b.qg, hidden_rows, b.sxb, b.rxb, 0, True, key_value_gradients)
        share_stat(c.spr0, b.spr0, b.sall0, c.sall0, NX - 1)

        def memory_zero(k):
            yp = kv_got(k)
            far_rows = b.mgc.at[pl.ds(2 * NX * yp, 2 * NX)]
            got(c.mgc, far_rows, yp)

            def into(lanes, block):
                total = block + far_rows[:, :, lanes].astype(F32)
                b.mgs[pl.ds(2 * NX * yp, 2 * NX), :, lanes] = total.astype(BF)

            memory_rows(yp, into)
            for sec in range(2):
                x_send(
                    c.rm,
                    lambda xp, sec=sec: b.mgs.at[(2 * yp + sec) * NX + xp],
                    b.rm.at[NX * yp + x],
                    sec,
                    1 - sec,
                    yp,
                )
            b.rm[NX * yp + x] = b.mgs[2 * NX * yp + x]

        each(0, NY, memory_zero)

        def grad_zero(k):
            yp = near(k)
            x_got(c.xb, b.rxb, yp, NX - 1)

            @pl.when(k == 1)
            def _():
                got(c.sall0, b.sall0.at[pl.ds(0, NY - 1)])

            b.t2[yp] = norm_gradient(yp, b.rxb, b.gain, b.x0, b.inv0, b.sall0, b.t1)

            @pl.when(k > 0)
            def _():
                copy(c.sgr0, b.t2.at[yp], b.sgr.at[y], 0, dev(0, x, yp)).start()

        each(0, NY, grad_zero)
        b.sgr[y] = b.t2[y]

    @pl.when(s == 1)
    def _():
        enc_start()
        small_start()
        enc_half()
        got(c.dsl, b.x0.at[pl.ds(0, NY - 1)])
        got(c.gain, b.gain_far)
        enc_whole()
        sl_start()
        pl.semaphore_wait(go, 1)
        for w in (K, V, O, Q):
            ring_send(w, 0)
        ring_next(1, K, V, O, Q)
        ring_next(2, K, V, O, Q)
        ring_next(3, K, V, O, Q)
        ring_got(K, 3)
        project(c.pk, enc_group, lambda a: times(K, a), b.s_k, b.r_k, b.own_k)
        ring_got(V, 3)
        project(c.pv, enc_group, lambda a: times(V, a), b.s_v, b.r_v, b.own_v)
        sl_got()
        for yp in range(NY):
            copy(c.c0, b.a0.at[NX * yp + x], b.c0.at[yp], 0, dev(0, x, y)).start()
        ring_got(O, 3)
        project(c.pag, dec_rows(b.a0), times_out_t, b.s_ag, b.r_ag, b.own_ag)
        def stream_one(k):
            yp = near(k)
            x_got(c.xa, b.rxa, yp, NX)
            rows = (b.x0[yp].astype(F32) + sum_x(b.rxa, yp)).astype(BF)
            b.x1[yp] = rows
            rows = rows.astype(F32)
            b.a1[NX * yp + x] = (rows * b.gain[0:1, :]).astype(BF)
            gather_x(yp)
            squares = rows * rows
            lanes = squares[:, :N]
            for f in range(1, SL // N):
                lanes += squares[:, f * N : (f + 1) * N]
            b.ss[y, yp] = lanes

        each(0, NY, stream_one)
        y_send(c.ss, lambda i: b.ss.at[y], b.ss, 1, 1)
        b.k[...] = projected(c.pk, b.r_k, b.own_k).astype(BF)
        b.v[...] = projected(c.pv, b.r_v, b.own_v).astype(BF)
        b.ag[...] = projected(c.pag, b.r_ag, b.own_ag).astype(BF)
        probability_gradient()
        ring_got(Q, 3)

        copy(c.x1, b.x1, b.x1, 0, dev(0, x, y)).start()
        y_send(c.por, lambda i: b.x1.at[i], b.por, 0, 0)
        got(c.ss, b.ss.at[pl.ds(0, NY - 1)])

        def inverse_one(yp):
            lanes = b.ss[0, yp] + b.ss[1, yp] + b.ss[2, yp] + b.ss[3, yp]
            inv = lax.rsqrt(jnp.sum(lanes, axis=-1, keepdims=True) * (1.0 / D) + EPS)
            b.inv1[yp] = jnp.broadcast_to(inv, (ROWS, N))

        each(0, NY, inverse_one)
        b.invx[x] = b.inv1[y]
        x_send(c.invx, lambda xp: b.inv1.at[y], b.invx.at[x], 1, 1)
        copy(c.inv1, b.inv1, b.inv1, 0, dev(0, x, y)).start()
        project(c.pq, dec_rows(b.a1), lambda a: times(Q, a), b.s_q, b.r_q, b.own_q, a1_got)
        got(c.invx, b.invx.at[pl.ds(0, NX - 1)])
        row_scale = b.invx[...].reshape(N, N) * SCALE
        row_scale = jnp.concatenate([row_scale] * (COLS // N), axis=1)
        b.q[...] = (projected(c.pq, b.r_q, b.own_q) * row_scale).astype(BF)
        probabilities()
        query_gradient()
        send_stat(c.spr1, b.spr1, False)
        scatter_x(c.xa, c.qg, b.qg, hidden_rows, b.sxa, b.rxa, 0, False)

        key_value_gradients()

        def memory_one(k):
            yp = kv_got(k)

            def into(lanes, block):
                b.mgs[pl.ds(2 * NX * yp, 2 * NX), :, lanes] = block.astype(BF)

            memory_rows(yp, into)
            rows = pl.ds(2 * NX * yp, 2 * NX)
            copy(c.mgc, b.mgs.at[rows], b.mgc.at[rows], yp, dev(0, x, y)).start()

        each(0, NY, memory_one)
        attend()
        scatter_x(c.xb, c.at, b.at, update_rows, b.sxb, b.rxb, 1, True)

        def output_one(k):
            yp = near(k)
            x_got(c.xb, b.rxb, yp, NX - 1)
            b.t2[yp] = (b.x1[yp].astype(F32) + sum_x(b.rxb, yp)).astype(BF)

        each(0, NY, output_one)
        y_send(c.por1, lambda i: b.t2.at[i], b.por, 1, 1)
        b.por[y] = b.t2[y]

    store_p = local(b.por, out_p, 10)
    store_s = local(b.sgr, out_s, 11)
    store_m = local(b.mo, out_m, 12)

    @pl.when(s == 0)
    def _():
        got(c.por, b.por)

    @pl.when(s == 1)
    def _():
        got(c.por1, b.por.at[pl.ds(0, NY - 1)])
        got(c.sgr, b.sgr)
        store_s.start()

    store_p.start()

    def memory_sum(k):
        yp = near(k)

        @pl.when(s == 0)
        def _():
            x_got(c.rm, b.rm, yp, NX - 1)

        @pl.when(s == 1)
        def _():
            x_got(c.rm, b.rm, yp, NX)

        b.mos[yp] = sum_x(b.rm, yp).astype(BF)

        @pl.when(k > 0)
        def _():
            copy(c.mo, b.mos.at[yp], b.mo.at[y], 0, dev(s, x, yp)).start()

    each(0, NY, memory_sum)
    b.mo[y] = b.mos[y]

    @pl.when(s == 0)
    def _():
        got(c.sgr0, b.sgr.at[pl.ds(0, NY - 1)])
        store_s.start()

    got(c.mo, b.mo.at[pl.ds(0, NY - 1)])
    store_m.start()

    three = pl.ds(0, NY - 1)
    for w in range(4):
        sent(rings[w], weights[w].at[pl.ds(0, NZ - 1)])
    sent(c.sl, b.a0.at[pl.ds(0, NXY - 1)])
    sent(c.enc, b.enc.at[pl.ds(0, NXY - 1)])
    sent(c.ehalf, b.enc.at[pl.ds(0, NXY)])
    sent(c.dsl, b.dsl.at[three])
    sent(c.gain, b.gain)
    for step in (c.pq, c.pk, c.pv, c.pag, c.at, c.qg, c.kg, c.vg):
        sent(step, b.s_q.at[three])
    sent(c.a1, b.a1.at[pl.ds(0, NXY - NY)])
    sent(c.xa, b.sxa)
    sent(c.xb, b.sxb.at[pl.ds(0, NXY - NY)])
    sent(c.mo, b.mos.at[three])

    @pl.when(s == 0)
    def _():
        sent(c.inv0, b.inv0.at[three])
        sent(c.sall1, b.sall1.at[three])
        sent(c.sall0, b.sall0.at[three])
        sent(c.spr0, b.sp.at[three])
        sent(c.sgr, b.t1)
        sent(c.sgr0, b.t2.at[three])
        sent(c.rm, b.mgs.at[pl.ds(0, 2 * NXY - NY)])

    @pl.when(s == 1)
    def _():
        sent(c.c0, b.c0)
        sent(c.x1, b.x1)
        sent(c.inv1, b.inv1)
        sent(c.mgc, b.mgs)
        sent(c.por, b.x1)
        sent(c.por1, b.t2.at[three])
        sent(c.ss, b.ss.at[three])
        sent(c.invx, b.invx.at[three])
        sent(c.spr1, b.sp)

    store_p.wait()
    store_s.wait()
    store_m.wait()


def assemble(phase, stream, memory, out_p, out_s, out_m):
    for source, out in ((phase, out_p), (stream, out_s), (memory, out_m)):
        for yp in range(NY):
            value = source[yp]
            for f in range(NZ):
                at = (NY * f + yp) * N
                out[:, at : at + N] = value[:, f * N : (f + 1) * N].astype(out.dtype)


def body(*args):
    dec, enc, dseg, eseg, gain, wq, wk, wv, wo, cot = args
    parts = pl.pallas_call(
        kernel,
        out_shape=(
            jax.ShapeDtypeStruct((NY, ROWS, SL), BF),
            jax.ShapeDtypeStruct((NY, ROWS, SL), BF),
            jax.ShapeDtypeStruct((NY, EROWS, SL), BF),
        ),
        in_specs=[pl.BlockSpec(memory_space=pl.ANY)] * 10,
        out_specs=(pl.BlockSpec(memory_space=pl.ANY),) * 3,
        scratch_shapes=list(BUFFERS.values())
        + [pltpu.SemaphoreType.DMA(shape) for shape in COPIES.values()]
        + [
            pltpu.SemaphoreType.DMA((len(COPIES),)),
            pltpu.SemaphoreType.DMA((LOCAL,)),
            pltpu.SemaphoreType.REGULAR,
        ],
        compiler_params=pltpu.CompilerParams(
            collective_id=0, has_side_effects=True, vmem_limit_bytes=56 * 2**20
        ),
        cost_estimate=pl.CostEstimate(
            flops=16 * 2**30, bytes_accessed=4 * 2**20, transcendentals=2**16
        ),
        name="decoder_phases",
    )(dec[0], enc[0], dseg, eseg, gain, wq[0], wk[0], wv[0], wo[0], cot[0])
    phase, stream, memory = pl.pallas_call(
        assemble,
        out_shape=(
            jax.ShapeDtypeStruct((ROWS, D), BF),
            jax.ShapeDtypeStruct((ROWS, D), BF),
            jax.ShapeDtypeStruct((EROWS, D), F32),
        ),
        in_specs=[pl.BlockSpec(memory_space=pltpu.VMEM)] * 3,
        out_specs=(pl.BlockSpec(memory_space=pltpu.VMEM),) * 3,
        name="assemble",
    )(*parts)
    return phase[None, None], stream[None, None], memory[None]


def solution(mesh):
    in_specs = (
        P("dp", "mp", None),
        P("dp", ("section", "mp"), None),
        P("dp", None),
        P("dp", None),
        P("section", None),
        P("section", "dp", "mp"),
        P("section", "dp", "mp"),
        P("section", "dp", "mp"),
        P("section", "mp", "dp"),
        P("dp", "mp", None),
    )
    out_specs = (
        P("section", "dp", "mp", None),
        P("section", "dp", "mp", None),
        P("dp", ("section", "mp"), None),
    )
    return jax.shard_map(body, mesh=mesh, in_specs=in_specs, out_specs=out_specs, check_vma=False)
```

```python
from types import SimpleNamespace

import jax
import jax.numpy as jnp
from jax import lax
from jax.experimental import pallas as pl
from jax.experimental.pallas import tpu as pltpu
from jax.sharding import PartitionSpec as P

MESH = pl.DeviceIdType.MESH
BF = jnp.bfloat16
F32 = jnp.float32

NX, NY, NZ = 4, 4, 8
NXY = NX * NY
D = 4096
DK = 256
COLS = 512
HEADS = COLS // DK
ROWS = 32
EROWS = 16
SL = D // NY
N = 128
EPS = 1e-06
SCALE = DK ** (-0.5)
STAT = 1.0 / (D * SCALE)
Q, K, V, O = range(4)
ORDER = (0, 1, 3, 2)


def vm(*shape, dtype=BF):
    return pltpu.VMEM(shape, dtype)


BUFFERS = dict(
    wq=vm(NZ, N, COLS),
    wk=vm(NZ, N, COLS),
    wv=vm(NZ, N, COLS),
    wo=vm(NZ, COLS, N),
    dec=vm(ROWS, D),
    enc_in=vm(EROWS, D),
    cot=vm(ROWS, D),
    gain_in=vm(1, D, dtype=F32),
    dseg=vm(1, N, dtype=jnp.int32),
    eseg=vm(1, N, dtype=jnp.int32),
    esl=vm(NY, EROWS, SL),
    enc=vm(2 * NXY, EROWS, SL),
    sl=vm(NY, ROWS, SL),
    a0=vm(NXY, ROWS, SL),
    a1=vm(NXY, ROWS, SL),
    dsl=vm(NY, ROWS, SL),
    x0=vm(NY, ROWS, SL),
    c0=vm(NY, ROWS, SL),
    x1=vm(NY, ROWS, SL),
    t1=vm(NY, ROWS, SL),
    t2=vm(NY, ROWS, SL),
    inv0s=vm(ROWS, N, dtype=F32),
    inv0=vm(NY, ROWS, N, dtype=F32),
    inv1=vm(NY, ROWS, N, dtype=F32),
    invx=vm(NX, ROWS, N, dtype=F32),
    gain=vm(8, SL, dtype=F32),
    gain_far=vm(8, SL, dtype=F32),
    mask=vm(N, N, dtype=F32),
    prob=vm(HEADS, N, N, dtype=F32),
    pg=vm(HEADS, N, N, dtype=F32),
    sgt=vm(HEADS, N, N),
    pt=vm(HEADS, N, N),
    q=vm(N, COLS),
    k=vm(N, COLS),
    v=vm(N, COLS),
    ag=vm(N, COLS),
    own_q=vm(N, COLS, dtype=F32),
    own_k=vm(N, COLS, dtype=F32),
    own_v=vm(N, COLS, dtype=F32),
    own_ag=vm(N, COLS, dtype=F32),
    s_q=vm(NY, N, COLS),
    s_k=vm(NY, N, COLS),
    s_v=vm(NY, N, COLS),
    s_ag=vm(NY, N, COLS),
    r_q=vm(NY, N, COLS),
    r_k=vm(NY, N, COLS),
    r_v=vm(NY, N, COLS),
    r_ag=vm(NY, N, COLS),
    at=vm(NY, N, COLS),
    qg=vm(NY, N, COLS),
    kg=vm(NY, N, COLS),
    vg=vm(NY, N, COLS),
    sxa=vm(NXY, ROWS, SL),
    sxb=vm(NXY, ROWS, SL),
    rxa=vm(NXY, ROWS, SL),
    rxb=vm(NXY, ROWS, SL),
    ss=vm(NY, NY, ROWS, N, dtype=F32),
    sp=vm(NX, ROWS, N, dtype=F32),
    spr1=vm(NX, ROWS, N, dtype=F32),
    spr0=vm(NX, ROWS, N, dtype=F32),
    sall1=vm(NY, ROWS, N, dtype=F32),
    sall0=vm(NY, ROWS, N, dtype=F32),
    por=vm(NY, ROWS, SL),
    sgr=vm(NY, ROWS, SL),
    mgs=vm(2 * NXY, EROWS, SL),
    mgc=vm(2 * NXY, EROWS, SL),
    rm=vm(NXY, EROWS, SL),
    mos=vm(NY, EROWS, SL),
    mo=vm(NY, EROWS, SL),
)

COPIES = dict(
    ring_q=(2, 4),
    ring_k=(2, 4),
    ring_v=(2, 4),
    ring_o=(2, 4),
    enc=(1,),
    sl=(1,),
    dsl=(1,),
    inv0=(1,),
    gain=(1,),
    ehalf=(1,),
    c0=(1,),
    pq=(1,),
    pk=(1,),
    pv=(1,),
    pag=(1,),
    at=(NY,),
    qg=(NY,),
    kg=(NY,),
    vg=(NY,),
    xa=(NY,),
    xb=(NY,),
    a1=(NY,),
    ss=(1,),
    invx=(1,),
    inv1=(1,),
    x1=(1,),
    spr1=(1,),
    spr0=(1,),
    sall1=(1,),
    sall0=(1,),
    por=(1,),
    por1=(1,),
    sgr=(1,),
    sgr0=(1,),
    mgc=(NY,),
    rm=(NY,),
    mo=(1,),
)
LOCAL = 13


def nn(a, b):
    return jnp.dot(a, b, preferred_element_type=F32)


def nt(a, b):
    return lax.dot_general(a, b, (((1,), (1,)), ((), ())), preferred_element_type=F32)


def kernel(*refs):
    dec, enc_in, dseg, eseg, gain_in, wq_in, wk_in, wv_in, wo_in, cot = refs[:10]
    out_p, out_s, out_m = refs[10:13]
    scratch = refs[13:]
    b = SimpleNamespace(**dict(zip(BUFFERS, scratch)))
    rest = scratch[len(BUFFERS) :]
    send_sems, local_sems, go = rest[len(COPIES) :]
    c = SimpleNamespace(**{n: (r, i) for i, (n, r) in enumerate(zip(COPIES, rest))})

    s = lax.axis_index("section")
    x = lax.axis_index("mp")
    dp = lax.axis_index("dp")
    y = dp % NY
    z = dp // NY
    far = 1 - s

    def dev(sec, xx, yy, zz=None):
        return {"section": sec, "mp": xx, "dp": (z if zz is None else zz) * NY + yy}

    here = dev(s, x, y)

    def copy(step, src, dst, at, device):
        return pltpu.make_async_remote_copy(
            src_ref=src,
            dst_ref=dst,
            send_sem=send_sems.at[step[1]],
            recv_sem=step[0].at[at],
            device_id=device,
            device_id_type=MESH,
        )

    def got(step, ref, at=0):
        copy(step, ref, ref, at, here).wait_recv()

    def sent(step, ref):
        first = (0,) * len(step[0].shape)
        copy(step, ref, ref, first, here).wait_send()

    def each(lo, hi, body):
        lax.fori_loop(lo, hi, lambda i, carry: (body(i), carry)[1], 0)

    def by_distance(i):
        return i + (i // 2) * (5 - 2 * i)

    def far_first(i):
        return (2 * i) % 3 + 3 * (i // 3)

    def near(k):
        return (y + by_distance(k)) % NY

    def y_send(step, src_of, dst, sec, lo, at=None):
        def one(k):
            yp = (y + k) % NY
            copy(step, src_of(yp), dst.at[y], 0 if at is None else at, dev(sec, x, yp)).start()

        each(lo, NY, one)

    def x_send(step, src_of, dst, sec, lo, at=0):
        def one(k):
            xp = (x + far_first(k)) % NX
            copy(step, src_of(xp), dst, at, dev(sec, xp, y)).start()

        each(lo, NX, one)

    weights = (b.wq, b.wk, b.wv, b.wo)
    rings = (c.ring_q, c.ring_k, c.ring_v, c.ring_o)

    def part(w, slot, step, way):
        ref = weights[w]
        if step < 3:
            return ref.at[slot]
        half = ref.shape[1] // 2
        return ref.at[slot, pl.ds(way * half, half)]

    def ring_send(w, step):
        for way in range(2):
            slot = (z + NZ - step) % NZ if way == 0 else (z + step) % NZ
            to = (z + 1) % NZ if way == 0 else (z + NZ - 1) % NZ
            ref = part(w, slot, step, way)
            copy(rings[w], ref, ref, (way, step), dev(s, x, y, to)).start()

    def ring_got(w, step):
        for way in range(2):
            slot = (z + NZ - 1 - step) % NZ if way == 0 else (z + 1 + step) % NZ
            got(rings[w], part(w, slot, step, way), (way, step))

    def ring_next(step, *ws):
        for w in ws:
            ring_got(w, step - 1)
            ring_send(w, step)

    barrier = pltpu.get_barrier_semaphore()

    def hello(device):
        pl.semaphore_signal(barrier, inc=1, device_id=device, device_id_type=MESH)

    def hello_xy(k):
        t = (NX * y + x + k) % NXY
        hello(dev(s, t % NX, t // NX))

    each(1, NXY, hello_xy)
    hello(dev(s, x, y, (z + 1) % NZ))
    hello(dev(s, x, y, (z + NZ - 1) % NZ))
    each(0, NX, lambda k: hello(dev(far, (x + k) % NX, y)))
    each(1, NY, lambda k: hello(dev(far, x, (y + k) % NY)))

    def local(src, dst, i):
        return pltpu.make_async_copy(src, dst, local_sems.at[i])

    loads = [
        local(src, dst, i)
        for i, (src, dst) in enumerate(
            (
                (dec, b.dec),
                (gain_in, b.gain_in),
                (enc_in, b.enc_in),
                (dseg, b.dseg),
                (eseg, b.eseg),
                (cot, b.cot),
                (wq_in, b.wq.at[z]),
                (wk_in, b.wk.at[z]),
                (wv_in, b.wv.at[z]),
                (wo_in, b.wo.at[z]),
            )
        )
    ]
    for load in loads:
        load.start()
    for load in loads:
        load.wait()

    def pick(value, yp):
        return jnp.concatenate(
            [value[:, (NY * f + yp) * N : (NY * f + yp + 1) * N] for f in range(NZ)], axis=1
        )

    rows_in = b.dec[...]
    enc_rows = b.enc_in[...]

    @pl.when(s == 0)
    def _():
        wide = rows_in.astype(F32)
        inverse = lax.rsqrt(jnp.mean(wide * wide, axis=-1, keepdims=True) + EPS)
        inv_tile = jnp.broadcast_to(inverse, (ROWS, N))
        b.inv0s[...] = inv_tile
        b.inv0[y] = inv_tile
        hidden = (wide * inverse * b.gain_in[...]).astype(BF)
        for yp in range(NY):
            b.sl[yp] = pick(hidden, yp)

    @pl.when(s == 1)
    def _():
        value = b.cot[...]
        for yp in range(NY):
            b.sl[yp] = pick(value, yp)

    for yp in range(NY):
        b.dsl[yp] = pick(rows_in, yp)
        b.esl[yp] = pick(enc_rows, yp)
    b.a0[NX * y + x] = b.sl[y]
    b.x0[y] = b.dsl[y]
    b.enc[(2 * y + s) * NX + x] = b.esl[y]
    for f in range(NZ):
        own_gain = b.gain_in[:, pl.ds(pl.multiple_of((NY * f + y) * N, N), N)]
        b.gain[:, f * N : (f + 1) * N] = jnp.broadcast_to(own_gain, (8, N))
    dec_ids = jnp.broadcast_to(b.dseg[...].astype(F32), (N, N)).T
    enc_ids = jnp.broadcast_to(b.eseg[...].astype(F32), (N, N))
    b.mask[...] = jnp.where(dec_ids == enc_ids, 1.0, 0.0)

    pl.semaphore_wait(barrier, NXY - 1 + 2 + NX + NY - 1)

    def xy_start(step, src, dst):
        def one(k):
            t = (NX * y + x + k) % NXY
            copy(step, src.at[t // NX], dst, 0, dev(s, t % NX, t // NX)).start()

        each(1, NXY, one)

    def enc_start():
        xy_start(c.enc, b.esl, b.enc.at[(2 * y + s) * NX + x])

    def sl_start():
        xy_start(c.sl, b.sl, b.a0.at[NX * y + x])

    def small_start():
        copy(c.gain, b.gain, b.gain_far, 0, dev(far, x, y)).start()
        y_send(c.dsl, lambda i: b.dsl.at[i], b.x0, s, 1)

    def enc_half():
        got(c.enc, b.enc.at[pl.ds(0, NXY - 1)])
        for yp in range(NY):
            block = b.enc.at[pl.ds((2 * yp + s) * NX, NX)]
            copy(c.ehalf, block, block, 0, dev(far, x, y)).start()

    def enc_whole():
        got(c.ehalf, b.enc.at[pl.ds(0, NXY)])

    def sl_got():
        got(c.sl, b.a0.at[pl.ds(0, NXY - 1)])

    def times(w, a):
        return nn(a, weights[w][...].reshape(NZ * N, COLS))

    def pair(p):
        return jnp.concatenate([b.wo[2 * p], b.wo[2 * p + 1]], axis=1)

    def times_out_t(a):
        total = nt(a[:, : 2 * N], pair(0))
        for p in range(1, NZ // 2):
            total += nt(a[:, 2 * N * p : 2 * N * (p + 1)], pair(p))
        return total

    def dec_rows(buffer):
        return lambda yp: buffer[pl.ds(NX * yp, NX)].reshape(N, SL)

    def enc_group(yp):
        return b.enc[pl.ds(2 * NX * yp, 2 * NX)].reshape(N, SL)

    def project(step, rows_of, product, stage, landing, own, arrived=None):
        def one(k):
            if arrived is not None:
                yp = near(k)
                arrived(yp)
            else:
                yp = (y + far_first(k)) % NY
            stage[yp] = product(rows_of(yp)).astype(BF)
            copy(step, stage.at[yp], landing.at[y], 0, dev(s, x, yp)).start()

        if arrived is not None:
            arrived(y)
            own[...] = product(rows_of(y))
            each(1, NY, one)
        else:
            each(1, NY, one)
            own[...] = product(rows_of(y))

    def projected(step, landing, own):
        got(step, landing.at[pl.ds(0, NY - 1)])
        total = own[...]
        for k in range(1, NY):
            total += landing[(y + k) % NY].astype(F32)
        return total

    def head(value, h):
        return value[:, h * DK : (h + 1) * DK]

    def probabilities():
        for h in range(HEADS):
            scores = nt(head(b.q, h), head(b.k, h))
            scores = jnp.where(b.mask[...] > 0.5, scores, -1e30)
            top = jnp.max(scores, axis=-1, keepdims=True)
            e = jnp.exp(scores - top)
            b.prob[h] = e / jnp.sum(e, axis=-1, keepdims=True)

    def gather_y(step, buffer):
        def one(k):
            copy(step, buffer.at[y], buffer.at[y], y, dev(s, x, near(k))).start()

        each(1, NY, one)

    def attend():
        b.at[y] = jnp.concatenate(
            [nn(b.prob[h].astype(BF), head(b.v, h)) for h in range(HEADS)], axis=1
        ).astype(BF)
        gather_y(c.at, b.at)

    def probability_gradient():
        for h in range(HEADS):
            b.pg[h] = nt(head(b.ag, h), head(b.v, h))

    def query_gradient():
        grads = []
        for h in range(HEADS):
            prob = b.prob[h]
            prob_grad = b.pg[h]
            score_grad = prob * (prob_grad - jnp.sum(prob_grad * prob, axis=-1, keepdims=True))
            b.sgt[h] = score_grad.T.astype(BF)
            grads.append(nn(score_grad.astype(BF), head(b.k, h)) * SCALE)
        low = jnp.concatenate(grads, axis=1).astype(BF)
        b.qg[y] = low
        gather_y(c.qg, b.qg)
        both = low.astype(F32) * b.q[...].astype(F32)
        lanes = both[:, :N]
        for f in range(1, COLS // N):
            lanes += both[:, f * N : (f + 1) * N]
        b.sp[...] = lanes.reshape(NX, ROWS, N)

    def key_value_gradients():
        for h in range(HEADS):
            b.pt[h] = b.prob[h].T.astype(BF)
        b.kg[y] = jnp.concatenate(
            [nn(b.sgt[h], head(b.q, h)) for h in range(HEADS)], axis=1
        ).astype(BF)
        gather_y(c.kg, b.kg)
        b.vg[y] = jnp.concatenate(
            [nn(b.pt[h], head(b.ag, h)) for h in range(HEADS)], axis=1
        ).astype(BF)
        gather_y(c.vg, b.vg)

    def update_rows(yp, stage):
        a = b.at[yp]
        for p in range(NZ // 2):
            part_out = nn(a, pair(p)).astype(BF).reshape(NX, ROWS, 2 * N)
            stage[pl.ds(NX * yp, NX), :, 2 * N * p : 2 * N * (p + 1)] = part_out

    def hidden_rows(yp, stage):
        a = b.qg[yp]
        for p in range(NZ // 2):
            block = b.wq[2 * p : 2 * p + 2].reshape(2 * N, COLS)
            part_out = nt(a, block).astype(BF).reshape(NX, ROWS, 2 * N)
            stage[pl.ds(NX * yp, NX), :, 2 * N * p : 2 * N * (p + 1)] = part_out

    def scatter_x(step, source_step, source, rows_into, stage, landing, sec, keep, then=None):
        def one(k):
            yp = near(k)

            if not isinstance(k, int):

                @pl.when(k > 0)
                def _():
                    got(source_step, source.at[yp], yp)

            rows_into(yp, stage)
            x_send(
                step,
                lambda xp: stage.at[NX * yp + xp],
                landing.at[NX * yp + x],
                sec,
                1 if keep else 0,
                yp,
            )
            if keep:
                landing[NX * yp + x] = stage[NX * yp + x]

        if then is None:
            each(0, NY, one)
        else:
            one(0)
            then()
            each(1, NY, one)

    def x_got(step, landing, yp, blocks):
        got(step, landing.at[pl.ds(NX * yp, blocks)], yp)

    def sum_x(landing, yp):
        total = landing[NX * yp].astype(F32)
        for i in range(1, NX):
            total += landing[NX * yp + i].astype(F32)
        return total

    def gather_x(yp):
        block = b.a1.at[NX * yp + x]
        x_send(c.a1, lambda xp: block, block, s, 1, yp)

    def a1_got(yp):
        x_got(c.a1, b.a1, yp, NX - 1)

    def across(tile):
        return jnp.concatenate([tile] * (SL // N), axis=1)

    def send_stat(step, landing, keep):
        x_send(step, lambda xp: b.sp.at[xp], landing.at[x], 0, 1 if keep else 0)
        if keep:
            landing[x] = b.sp[x]

    def share_stat(step, landing, result, step_out, blocks):
        got(step, landing.at[pl.ds(0, blocks)])
        lanes = landing[0] + landing[1] + landing[2] + landing[3]
        result[y] = jnp.broadcast_to(jnp.sum(lanes, axis=-1, keepdims=True), (ROWS, N))
        y_send(step_out, lambda i: result.at[y], result, 0, 1)

    def norm_gradient(yp, landing, gain_ref, rows, inv_ref, stat_ref, grad):
        u = sum_x(landing, yp) * gain_ref[0:1, :]
        inv = inv_ref[yp]
        coef = inv * inv * stat_ref[yp] * STAT
        wide_rows = rows[yp].astype(F32)
        return (grad[yp].astype(F32) + across(inv) * u - wide_rows * across(coef)).astype(BF)

    def memory_rows(yp, into):
        key = b.kg[yp]
        value = b.vg[yp]
        for p in range(NZ // 2):
            wk_block = b.wk[2 * p : 2 * p + 2].reshape(2 * N, COLS)
            wv_block = b.wv[2 * p : 2 * p + 2].reshape(2 * N, COLS)
            block = (nt(key, wk_block) + nt(value, wv_block)).reshape(2 * NX, EROWS, 2 * N)
            into(slice(2 * N * p, 2 * N * (p + 1)), block)

    def kv_got(k):
        yp = near(k)

        @pl.when(k > 0)
        def _():
            got(c.kg, b.kg.at[yp], yp)
            got(c.vg, b.vg.at[yp], yp)

        return yp

    @pl.when(s == 0)
    def _():
        for w in (Q, K, V):
            ring_send(w, 0)
        enc_start()
        sl_start()
        ring_next(1, Q, K, V)
        small_start()
        y_send(c.inv0, lambda i: b.inv0s, b.inv0, 0, 1)
        ring_next(2, Q, K, V)
        ring_send(O, 0)
        enc_half()
        ring_next(3, Q, K, V)
        pl.semaphore_signal(go, inc=1, device_id=dev(1, x, y), device_id_type=MESH)
        ring_next(1, O)
        sl_got()
        ring_got(Q, 3)
        project(c.pq, dec_rows(b.a0), lambda a: times(Q, a), b.s_q, b.r_q, b.own_q)
        ring_next(2, O)
        enc_whole()
        ring_got(K, 3)
        project(c.pk, enc_group, lambda a: times(K, a), b.s_k, b.r_k, b.own_k)
        ring_next(3, O)
        ring_got(V, 3)
        project(c.pv, enc_group, lambda a: times(V, a), b.s_v, b.r_v, b.own_v)
        b.q[...] = (projected(c.pq, b.r_q, b.own_q) * SCALE).astype(BF)
        b.k[...] = projected(c.pk, b.r_k, b.own_k).astype(BF)
        probabilities()
        b.v[...] = projected(c.pv, b.r_v, b.own_v).astype(BF)
        attend()
        ring_got(O, 3)
        scatter_x(c.xa, c.at, b.at, update_rows, b.sxa, b.rxa, 1, False)

        got(c.gain, b.gain_far)
        got(c.c0, b.c0)
        got(c.dsl, b.x0.at[pl.ds(0, NY - 1)])
        got(c.inv0, b.inv0.at[pl.ds(0, NY - 1)])
        got(c.x1, b.x1)
        got(c.inv1, b.inv1)
        share_stat(c.spr1, b.spr1, b.sall1, c.sall1, NX)

        def grad_one(k):
            yp = near(k)
            x_got(c.xa, b.rxa, yp, NX)

            @pl.when(k == 1)
            def _():
                got(c.sall1, b.sall1.at[pl.ds(0, NY - 1)])

            g = norm_gradient(yp, b.rxa, b.gain_far, b.x1, b.inv1, b.sall1, b.c0)
            b.t1[yp] = g
            b.a1[NX * yp + x] = g
            gather_x(yp)

        each(0, NY, grad_one)
        y_send(c.sgr, lambda i: b.t1.at[i], b.sgr, 1, 0)

        project(c.pag, dec_rows(b.a1), times_out_t, b.s_ag, b.r_ag, b.own_ag, a1_got)
        b.ag[...] = projected(c.pag, b.r_ag, b.own_ag).astype(BF)
        probability_gradient()
        query_gradient()
        send_stat(c.spr0, b.spr0, True)
        scatter_x(c.xb, c.qg, b.qg, hidden_rows, b.sxb, b.rxb, 0, True, key_value_gradients)
        share_stat(c.spr0, b.spr0, b.sall0, c.sall0, NX - 1)

        def memory_zero(k):
            yp = kv_got(k)
            far_rows = b.mgc.at[pl.ds(2 * NX * yp, 2 * NX)]
            got(c.mgc, far_rows, yp)

            def into(lanes, block):
                total = block + far_rows[:, :, lanes].astype(F32)
                b.mgs[pl.ds(2 * NX * yp, 2 * NX), :, lanes] = total.astype(BF)

            memory_rows(yp, into)
            for sec in range(2):
                x_send(
                    c.rm,
                    lambda xp, sec=sec: b.mgs.at[(2 * yp + sec) * NX + xp],
                    b.rm.at[NX * yp + x],
                    sec,
                    1 - sec,
                    yp,
                )
            b.rm[NX * yp + x] = b.mgs[2 * NX * yp + x]

        each(0, NY, memory_zero)

        def grad_zero(k):
            yp = near(k)
            x_got(c.xb, b.rxb, yp, NX - 1)

            @pl.when(k == 1)
            def _():
                got(c.sall0, b.sall0.at[pl.ds(0, NY - 1)])

            b.t2[yp] = norm_gradient(yp, b.rxb, b.gain, b.x0, b.inv0, b.sall0, b.t1)

            @pl.when(k > 0)
            def _():
                copy(c.sgr0, b.t2.at[yp], b.sgr.at[y], 0, dev(0, x, yp)).start()

        each(0, NY, grad_zero)
        b.sgr[y] = b.t2[y]

    @pl.when(s == 1)
    def _():
        enc_start()
        small_start()
        enc_half()
        got(c.dsl, b.x0.at[pl.ds(0, NY - 1)])
        got(c.gain, b.gain_far)
        enc_whole()
        sl_start()
        pl.semaphore_wait(go, 1)
        for w in (K, V, O, Q):
            ring_send(w, 0)
        ring_next(1, K, V, O, Q)
        ring_next(2, K, V, O, Q)
        ring_next(3, K, V, O, Q)
        ring_got(K, 3)
        project(c.pk, enc_group, lambda a: times(K, a), b.s_k, b.r_k, b.own_k)
        ring_got(V, 3)
        project(c.pv, enc_group, lambda a: times(V, a), b.s_v, b.r_v, b.own_v)
        sl_got()
        for yp in range(NY):
            copy(c.c0, b.a0.at[NX * yp + x], b.c0.at[yp], 0, dev(0, x, y)).start()
        ring_got(O, 3)
        project(c.pag, dec_rows(b.a0), times_out_t, b.s_ag, b.r_ag, b.own_ag)
        def stream_one(k):
            yp = near(k)
            x_got(c.xa, b.rxa, yp, NX)
            rows = (b.x0[yp].astype(F32) + sum_x(b.rxa, yp)).astype(BF)
            b.x1[yp] = rows
            rows = rows.astype(F32)
            b.a1[NX * yp + x] = (rows * b.gain[0:1, :]).astype(BF)
            gather_x(yp)
            squares = rows * rows
            lanes = squares[:, :N]
            for f in range(1, SL // N):
                lanes += squares[:, f * N : (f + 1) * N]
            b.ss[y, yp] = lanes

        each(0, NY, stream_one)
        y_send(c.ss, lambda i: b.ss.at[y], b.ss, 1, 1)
        b.k[...] = projected(c.pk, b.r_k, b.own_k).astype(BF)
        b.v[...] = projected(c.pv, b.r_v, b.own_v).astype(BF)
        b.ag[...] = projected(c.pag, b.r_ag, b.own_ag).astype(BF)
        probability_gradient()
        ring_got(Q, 3)

        copy(c.x1, b.x1, b.x1, 0, dev(0, x, y)).start()
        y_send(c.por, lambda i: b.x1.at[i], b.por, 0, 0)
        got(c.ss, b.ss.at[pl.ds(0, NY - 1)])

        def inverse_one(yp):
            lanes = b.ss[0, yp] + b.ss[1, yp] + b.ss[2, yp] + b.ss[3, yp]
            inv = lax.rsqrt(jnp.sum(lanes, axis=-1, keepdims=True) * (1.0 / D) + EPS)
            b.inv1[yp] = jnp.broadcast_to(inv, (ROWS, N))

        each(0, NY, inverse_one)
        b.invx[x] = b.inv1[y]
        x_send(c.invx, lambda xp: b.inv1.at[y], b.invx.at[x], 1, 1)
        copy(c.inv1, b.inv1, b.inv1, 0, dev(0, x, y)).start()
        project(c.pq, dec_rows(b.a1), lambda a: times(Q, a), b.s_q, b.r_q, b.own_q, a1_got)
        got(c.invx, b.invx.at[pl.ds(0, NX - 1)])
        row_scale = b.invx[...].reshape(N, N) * SCALE
        row_scale = jnp.concatenate([row_scale] * (COLS // N), axis=1)
        b.q[...] = (projected(c.pq, b.r_q, b.own_q) * row_scale).astype(BF)
        probabilities()
        query_gradient()
        send_stat(c.spr1, b.spr1, False)
        scatter_x(c.xa, c.qg, b.qg, hidden_rows, b.sxa, b.rxa, 0, False)

        key_value_gradients()

        def memory_one(k):
            yp = kv_got(k)

            def into(lanes, block):
                b.mgs[pl.ds(2 * NX * yp, 2 * NX), :, lanes] = block.astype(BF)

            memory_rows(yp, into)
            rows = pl.ds(2 * NX * yp, 2 * NX)
            copy(c.mgc, b.mgs.at[rows], b.mgc.at[rows], yp, dev(0, x, y)).start()

        each(0, NY, memory_one)
        attend()
        scatter_x(c.xb, c.at, b.at, update_rows, b.sxb, b.rxb, 1, True)

        def output_one(k):
            yp = near(k)
            x_got(c.xb, b.rxb, yp, NX - 1)
            b.t2[yp] = (b.x1[yp].astype(F32) + sum_x(b.rxb, yp)).astype(BF)

        each(0, NY, output_one)
        y_send(c.por1, lambda i: b.t2.at[i], b.por, 1, 1)
        b.por[y] = b.t2[y]

    store_p = local(b.por, out_p, 10)
    store_s = local(b.sgr, out_s, 11)
    store_m = local(b.mo, out_m, 12)

    @pl.when(s == 0)
    def _():
        got(c.por, b.por)

    @pl.when(s == 1)
    def _():
        got(c.por1, b.por.at[pl.ds(0, NY - 1)])
        got(c.sgr, b.sgr)
        store_s.start()

    store_p.start()

    def memory_sum(k):
        yp = near(k)

        @pl.when(s == 0)
        def _():
            x_got(c.rm, b.rm, yp, NX - 1)

        @pl.when(s == 1)
        def _():
            x_got(c.rm, b.rm, yp, NX)

        b.mos[yp] = sum_x(b.rm, yp).astype(BF)

        @pl.when(k > 0)
        def _():
            copy(c.mo, b.mos.at[yp], b.mo.at[y], 0, dev(s, x, yp)).start()

    each(0, NY, memory_sum)
    b.mo[y] = b.mos[y]

    @pl.when(s == 0)
    def _():
        got(c.sgr0, b.sgr.at[pl.ds(0, NY - 1)])
        store_s.start()

    got(c.mo, b.mo.at[pl.ds(0, NY - 1)])
    store_m.start()

    three = pl.ds(0, NY - 1)
    for w in range(4):
        sent(rings[w], weights[w].at[pl.ds(0, NZ - 1)])
    sent(c.sl, b.a0.at[pl.ds(0, NXY - 1)])
    sent(c.enc, b.enc.at[pl.ds(0, NXY - 1)])
    sent(c.ehalf, b.enc.at[pl.ds(0, NXY)])
    sent(c.dsl, b.dsl.at[three])
    sent(c.gain, b.gain)
    for step in (c.pq, c.pk, c.pv, c.pag, c.at, c.qg, c.kg, c.vg):
        sent(step, b.s_q.at[three])
    sent(c.a1, b.a1.at[pl.ds(0, NXY - NY)])
    sent(c.xa, b.sxa)
    sent(c.xb, b.sxb.at[pl.ds(0, NXY - NY)])
    sent(c.mo, b.mos.at[three])

    @pl.when(s == 0)
    def _():
        sent(c.inv0, b.inv0.at[three])
        sent(c.sall1, b.sall1.at[three])
        sent(c.sall0, b.sall0.at[three])
        sent(c.spr0, b.sp.at[three])
        sent(c.sgr, b.t1)
        sent(c.sgr0, b.t2.at[three])
        sent(c.rm, b.mgs.at[pl.ds(0, 2 * NXY - NY)])

    @pl.when(s == 1)
    def _():
        sent(c.c0, b.c0)
        sent(c.x1, b.x1)
        sent(c.inv1, b.inv1)
        sent(c.mgc, b.mgs)
        sent(c.por, b.x1)
        sent(c.por1, b.t2.at[three])
        sent(c.ss, b.ss.at[three])
        sent(c.invx, b.invx.at[three])
        sent(c.spr1, b.sp)

    store_p.wait()
    store_s.wait()
    store_m.wait()


def assemble(phase, stream, memory, out_p, out_s, out_m):
    for source, out in ((phase, out_p), (stream, out_s), (memory, out_m)):
        for yp in range(NY):
            value = source[yp]
            for f in range(NZ):
                at = (NY * f + yp) * N
                out[:, at : at + N] = value[:, f * N : (f + 1) * N].astype(out.dtype)


def body(*args):
    dec, enc, dseg, eseg, gain, wq, wk, wv, wo, cot = args
    parts = pl.pallas_call(
        kernel,
        out_shape=(
            jax.ShapeDtypeStruct((NY, ROWS, SL), BF),
            jax.ShapeDtypeStruct((NY, ROWS, SL), BF),
            jax.ShapeDtypeStruct((NY, EROWS, SL), BF),
        ),
        in_specs=[pl.BlockSpec(memory_space=pl.ANY)] * 10,
        out_specs=(pl.BlockSpec(memory_space=pl.ANY),) * 3,
        scratch_shapes=list(BUFFERS.values())
        + [pltpu.SemaphoreType.DMA(shape) for shape in COPIES.values()]
        + [
            pltpu.SemaphoreType.DMA((len(COPIES),)),
            pltpu.SemaphoreType.DMA((LOCAL,)),
            pltpu.SemaphoreType.REGULAR,
        ],
        compiler_params=pltpu.CompilerParams(
            collective_id=0, has_side_effects=True, vmem_limit_bytes=56 * 2**20
        ),
        cost_estimate=pl.CostEstimate(
            flops=16 * 2**30, bytes_accessed=4 * 2**20, transcendentals=2**16
        ),
        name="decoder_phases",
    )(dec[0], enc[0], dseg, eseg, gain, wq[0], wk[0], wv[0], wo[0], cot[0])
    phase, stream, memory = pl.pallas_call(
        assemble,
        out_shape=(
            jax.ShapeDtypeStruct((ROWS, D), BF),
            jax.ShapeDtypeStruct((ROWS, D), BF),
            jax.ShapeDtypeStruct((EROWS, D), F32),
        ),
        in_specs=[pl.BlockSpec(memory_space=pltpu.VMEM)] * 3,
        out_specs=(pl.BlockSpec(memory_space=pltpu.VMEM),) * 3,
        name="assemble",
    )(*parts)
    return phase[None, None], stream[None, None], memory[None]


def solution(mesh):
    in_specs = (
        P("dp", "mp", None),
        P("dp", ("section", "mp"), None),
        P("dp", None),
        P("dp", None),
        P("section", None),
        P("section", "dp", "mp"),
        P("section", "dp", "mp"),
        P("section", "dp", "mp"),
        P("section", "mp", "dp"),
        P("dp", "mp", None),
    )
    out_specs = (
        P("section", "dp", "mp", None),
        P("section", "dp", "mp", None),
        P("dp", ("section", "mp"), None),
    )
    return jax.shard_map(body, mesh=mesh, in_specs=in_specs, out_specs=out_specs, check_vma=False)
```
